32 devices in a mesh: groups: 2 (over x), src: 16 (over z, y, core).
Axes of the slice: x: 2, y: 2, z: 4, core: 2. Of those that a mesh axis runs over, the one named last changes fastest.
Arguments:
- source_feats: float32 [3072, 128], P(('groups', 'src')), parts along dimension 0, may hold values from -5 to 5, as said below
- target_feats: float32 [4096, 128], P(('groups', 'src')), parts along dimension 0, may hold values from -5 to 5, as said below
- log_a: float32 [3072], P(('groups', 'src')), parts along dimension 0, may hold values from -1 to 1
- log_b: float32 [4096], P(('groups', 'src')), parts along dimension 0, may hold values from -1 to 1
Outputs:
- f_pot: float32 [3072], P(('groups', 'src')), parts along dimension 0
- g_pot: float32 [4096], P(('groups', 'src')), parts along dimension 0
- src_moved: float32 [3072, 128], P(('groups', 'src')), parts along dimension 0
- tgt_moved: float32 [4096, 128], P(('groups', 'src')), parts along dimension 0
The draws below stay inside these ranges and needn't reach their ends.
There are 2 independent parts, one for each index of `groups`. The reference program is written for one: setup_inputs(seed, part) draws one part's arguments, and reference() takes and returns one part's arrays. A program takes and returns all parts, laid end to end along the dimension named above; each array names one. Nothing has to cross between parts.
Inputs may be any that keep to these rules, and one draw needn't show every extreme that they name: `source_feats`: entries are real-valued features. `target_feats`: entries are real-valued features.
All inputs are finite; a program needn't handle non-finite values.
Results may differ from the reference program's by a relative error of at most 0.0003.
Values sent between devices are 32-bit elements; how exact they have to be, the bound alone decides.
No kernel may reach another device: no remote copies, remote signals or barrier semaphores. Data moves between devices by JAX's collectives and lax.ppermute only.
A program may use at most 128 MiB of HBM per device.

```python
import jax
import jax.numpy as jnp
from jax import lax

FEAT = 128
S_DEV = 96
ITERS = 3
SOURCES = 1536
TARGETS = 2048
N_SRC = 16


def feature_rows(key, count, width):
    values = jax.random.normal(jax.random.fold_in(key, 14), (count, width), jnp.float32)
    return jnp.clip(values, -5.0, 5.0)


def draw_source_feats(key, part):
    return feature_rows(jax.random.fold_in(key, 101), SOURCES, FEAT)


def draw_target_feats(key, part):
    return feature_rows(jax.random.fold_in(key, 202), TARGETS, FEAT)


def levels(key, dims, split, smallest, top_value):
    factor_of, own = 1.0, jax.random.fold_in(key, 6)
    for position, parts in split:
        heights = jnp.exp(jax.random.uniform(jax.random.fold_in(own, position), (parts,), jnp.float32, smallest / len(split), top_value / len(split)))
        factor_of = factor_of * jnp.repeat(heights, dims[position] // parts).reshape([-1 if axis == position else 1 for axis in range(len(dims))])
    return factor_of


def setup_inputs(seed: int = 0, part: int = 0) -> dict:
    arg_keys = jax.random.split(jax.random.key(seed), 5)
    part_keys = jax.random.split(jax.random.fold_in(arg_keys[4], part), 5)
    source_feats = draw_source_feats(jax.random.fold_in(jax.random.fold_in(arg_keys[4], part), 71), part)
    target_feats = draw_target_feats(jax.random.fold_in(jax.random.fold_in(arg_keys[4], part), 71), part)
    log_a = jnp.clip(jax.random.uniform(part_keys[2], (SOURCES,), jnp.float32, -1.0, 1.0) * levels(part_keys[2], (SOURCES,), ((0, 16),), -0.4, 0.0), -1.0, 1.0)
    log_b = jnp.clip(jax.random.uniform(part_keys[3], (TARGETS,), jnp.float32, -1.0, 1.0) * levels(part_keys[3], (TARGETS,), ((0, 16),), -0.4, 0.0), -1.0, 1.0)
    return {"source_feats": source_feats, "target_feats": target_feats, "log_a": log_a, "log_b": log_b}


EPS = 0.05


def pair_cost(rows, cols, rows_sq, cols_sq, width):
    inner = jnp.dot(rows, cols.T, precision=lax.Precision.HIGHEST, preferred_element_type=jnp.float32)
    return (rows_sq[:, None] + cols_sq[None, :] - 2.0 * inner) / width


def row_update(cost, g_pot, log_mass):
    scores = (g_pot[None, :] - cost) / EPS
    top = jnp.max(scores, axis=1)
    total = jnp.sum(jnp.exp(scores - top[:, None]), axis=1)
    return EPS * log_mass - EPS * (top + jnp.log(total))


def reference(source_feats, target_feats, log_a, log_b):
    width = source_feats.shape[1]
    blocks_x = source_feats.reshape(N_SRC, S_DEV, width)
    blocks_a = log_a.reshape(N_SRC, S_DEV)
    sq_tgt = jnp.sum(target_feats * target_feats, axis=1)

    def block_cost(xb):
        return pair_cost(xb, target_feats, jnp.sum(xb * xb, axis=1), sq_tgt, width)

    g_pot = jnp.zeros((TARGETS,), jnp.float32)
    f_blocks = jnp.zeros((N_SRC, S_DEV), jnp.float32)
    for step in range(ITERS):
        f_blocks = lax.map(lambda pair: row_update(block_cost(pair[0]), g_pot, pair[1]), (blocks_x, blocks_a))

        def column(carry, pair):
            top, total = carry
            xb, fb = pair
            scores = (fb[:, None] - block_cost(xb)) / EPS
            new_top = jnp.maximum(top, jnp.max(scores, axis=0))
            total = total * jnp.exp(top - new_top) + jnp.sum(jnp.exp(scores - new_top[None, :]), axis=0)
            return (new_top, total), None

        start = (jnp.full((TARGETS,), -jnp.inf, jnp.float32), jnp.zeros((TARGETS,), jnp.float32))
        (top, total), unused = lax.scan(column, start, (blocks_x, f_blocks))
        g_pot = EPS * log_b - EPS * (top + jnp.log(total))

    def final(acc, pair):
        xb, fb = pair
        plan = jnp.exp((fb[:, None] + g_pot[None, :] - block_cost(xb)) / EPS)
        carried = jnp.dot(plan, target_feats, precision=lax.Precision.HIGHEST, preferred_element_type=jnp.float32)
        moved = carried / jnp.sum(plan, axis=1)[:, None]
        acc = acc + lax.dot_general(plan, xb, (((0,), (0,)), ((), ())), precision=lax.Precision.HIGHEST, preferred_element_type=jnp.float32)
        return acc, moved

    acc, moved_blocks = lax.scan(final, jnp.zeros((TARGETS, width), jnp.float32), (blocks_x, f_blocks))
    f_pot = f_blocks.reshape(SOURCES)
    src_moved = moved_blocks.reshape(SOURCES, width)
    tgt_moved = acc / jnp.exp(log_b)[:, None]
    return (f_pot, g_pot, src_moved, tgt_moved)
```

```python
import functools

import jax
import jax.numpy as jnp
from jax import lax
from jax.experimental import pallas as pl
from jax.experimental.pallas import tpu as pltpu
from jax.sharding import PartitionSpec as P

ITERS = 3
EPS = 0.05
LN2 = 0.6931471805599453
LOG2E = 1.4426950408889634
SAFE = 2.0**30
REPLICATED_BYTES = 24 * 2**20
HI = lax.Precision.HIGHEST


def split3(a):
    first = a.astype(jnp.bfloat16)
    rest = a - first.astype(jnp.float32)
    second = rest.astype(jnp.bfloat16)
    third = (rest - second.astype(jnp.float32)).astype(jnp.bfloat16)
    return first, second, third


def nt_dot(a, b, precision=None):
    return lax.dot_general(
        a, b, (((1,), (1,)), ((), ())), precision=precision, preferred_element_type=jnp.float32
    )


def whole_group_kernel(n, s_dev, t_dev, blk, *refs):
    pieces = refs[: -13]
    f_ref, g_ref, sm_ref, tm_ref = refs[-13:-9]
    e_ref, xs, ys, la_col, u_col, fm, rows_p, cols_p, acc = refs[-9:]
    feat = pieces[0].shape[1]
    rows = s_dev + t_dev + 8
    k = LOG2E / (feat * EPS)
    sources, targets = n * s_dev, n * t_dev

    blocks = [(ref, at) for ref in pieces for at in range(0, ref.shape[0], rows)]
    las, lbs, g1s = [], [], []
    ones = jnp.ones((8, feat), jnp.float32)
    for d, (ref, at) in enumerate(blocks):
        x1, x2, x3 = split3(ref[at : at + s_dev, :] * (2.0 * k))
        xs[d * s_dev : (d + 1) * s_dev, :] = jnp.concatenate([x1, x1, x2, x2, x1, x3], 1)
        y = ref[at + s_dev : at + s_dev + t_dev, :]
        y1, y2, y3 = split3(y)
        ys[d * t_dev : (d + 1) * t_dev, :] = jnp.concatenate([y1, y2, y1, y2, y3, y1], 1)
        g1s.append(nt_dot(ones, y * y, HI)[0:1, :])
        lbs.append(ref[at + s_dev + t_dev : at + s_dev + t_dev + 1, :])
        las.append(ref[at + s_dev + t_dev + 1 : at + s_dev + t_dev + 2, :])
    g1 = jnp.concatenate(g1s, 1) * (-k)
    mass_b = jnp.exp(jnp.concatenate(lbs, 1))
    la_t = jnp.exp(jnp.concatenate(las, 0)).T
    for d in range(n):
        la_col[d * s_dev : (d + 1) * s_dev, :] = la_t[:s_dev, d : d + 1]

    steps = sources // blk

    def at_block(i):
        return pl.ds(pl.multiple_of(i * blk, blk), blk)

    def column_part(e, u):
        return jnp.sum((e * u).reshape(blk // 8, 8, targets), axis=0)

    def first(i, state):
        low, high = state
        s = at_block(i)
        t = nt_dot(xs[s, :], ys[...]) + g1
        top = jnp.max(t, axis=1, keepdims=True)
        e = jnp.exp2(t - top)
        e_ref[s, :] = e
        r = jnp.sum(e, axis=1, keepdims=True)
        u = la_col[s, :] / r
        fm[s, :] = top
        acc[...] += column_part(e, u)
        return low, high

    def later(v, i, state):
        low, high = state
        s = at_block(i)
        e = e_ref[s, :]
        r = jnp.sum(e * v, axis=1, keepdims=True)
        u = la_col[s, :] / r
        u_col[s, :] = u
        acc[...] += column_part(e, u)
        return jnp.minimum(low, r), jnp.maximum(high, r)

    v = None
    low, high = jnp.ones((blk, 1), jnp.float32), jnp.ones((blk, 1), jnp.float32)
    worst_low, worst_high = jnp.ones((1, targets), jnp.float32), jnp.ones((1, targets), jnp.float32)
    for step in range(ITERS):
        acc[...] = jnp.zeros_like(acc)
        body = first if step == 0 else functools.partial(later, v)
        low, high = lax.fori_loop(0, steps, body, (low, high))
        total = jnp.sum(acc[...], axis=0, keepdims=True)
        worst_low = jnp.minimum(worst_low, total)
        worst_high = jnp.maximum(worst_high, total)
        v = mass_b / total
    safe = (
        (jnp.min(low) > 1.0 / SAFE)
        & (jnp.max(high) < SAFE)
        & (jnp.min(worst_low) > 1.0 / SAFE)
        & (jnp.max(worst_high) < SAFE)
    )

    x_own = pieces[0][0:s_dev, :]
    sq_own = k * jnp.sum(x_own * x_own, axis=1, keepdims=True)

    @pl.when(safe)
    def _():
        u_own = u_col[0:s_dev, :]
        f_ref[...] = EPS * jnp.log(u_own) + (EPS * LN2) * (sq_own - fm[0:s_dev, :])
        g_ref[...] = EPS * jnp.log(v[:, 0:t_dev])
        rows_p[...] = e_ref[0:s_dev, :] * v
        cols_p[...] = e_ref[:, 0:t_dev] * u_col[...] * (1.0 / total[:, 0:t_dev])

    @pl.when(jnp.logical_not(safe))
    def _():
        log_b = jnp.log2(mass_b)

        def inner(i, carry):
            s = at_block(i)
            e_ref[s, :] = nt_dot(xs[s, :], ys[...])
            return carry

        lax.fori_loop(0, steps, inner, 0)

        def potentials(step, g):
            def row(i, carry):
                s = at_block(i)
                t = e_ref[s, :] + g
                top = jnp.max(t, axis=1, keepdims=True)
                total = jnp.sum(jnp.exp2(t - top), axis=1, keepdims=True)
                fm[s, :] = jnp.log2(la_col[s, :]) - top - jnp.log2(total)
                return carry

            lax.fori_loop(0, steps, row, 0)

            def column_top(i, top):
                s = at_block(i)
                return jnp.maximum(top, jnp.max(e_ref[s, :] + fm[s, :], axis=0, keepdims=True))

            top = lax.fori_loop(0, steps, column_top, jnp.full((1, targets), -jnp.inf, jnp.float32))

            def column_total(i, total):
                s = at_block(i)
                e = jnp.exp2(e_ref[s, :] + fm[s, :] - top)
                return total + jnp.sum(e, axis=0, keepdims=True)

            total = lax.fori_loop(0, steps, column_total, jnp.zeros((1, targets), jnp.float32))
            return log_b - top - jnp.log2(total)

        g = lax.fori_loop(0, ITERS, potentials, g1)
        f_ref[...] = (EPS * LN2) * (fm[0:s_dev, :] + sq_own)
        g_ref[...] = (EPS * LN2) * (g[:, 0:t_dev] - g1[:, 0:t_dev])
        rows_p[...] = jnp.exp2(e_ref[0:s_dev, :] + fm[0:s_dev, :] + g)
        own = jnp.exp2(e_ref[:, 0:t_dev] + fm[...] + g[:, 0:t_dev])
        cols_p[...] = own * (1.0 / mass_b[:, 0:t_dev])

    plan_rows = rows_p[...]
    mass = jnp.sum(plan_rows, axis=1, keepdims=True)
    p1, p2, p3 = split3(plan_rows)
    y1, y2, y3 = ys[:, 0:feat], ys[:, feat : 2 * feat], ys[:, 4 * feat : 5 * feat]

    def nn(a, b):
        return jnp.dot(a, b, preferred_element_type=jnp.float32)

    moved = nn(p1, y1) + ((nn(p1, y2) + nn(p2, y1)) + (nn(p2, y2) + nn(p1, y3) + nn(p3, y1)))
    sm_ref[...] = moved / mass

    def tn(a, b):
        return lax.dot_general(a, b, (((0,), (0,)), ((), ())), preferred_element_type=jnp.float32)

    q1, q2, q3 = split3(cols_p[...])
    x1, x2, x3 = xs[:, 0:feat], xs[:, 2 * feat : 3 * feat], xs[:, 5 * feat : 6 * feat]
    moved = tn(q1, x1) + ((tn(q1, x2) + tn(q2, x1)) + (tn(q2, x2) + tn(q1, x3) + tn(q3, x1)))
    tm_ref[...] = moved * (1.0 / (2.0 * k))


def exchange(block, axis):
    n = lax.axis_size(axis)

    def swap(a, bits):
        return lax.ppermute(a, axis, [(i, i ^ bits) for i in range(n)])

    far = [swap(block, bits) for bits in range(4, n, 4)]
    line = [block] + far
    side = [swap(a, 2) for a in line]
    mine = jnp.concatenate(line + side, axis=0)
    return [mine, swap(mine, 1)]


def per_device_whole(source_feats, target_feats, log_a, log_b):
    n = lax.axis_size("src")
    s_dev, feat = source_feats.shape
    t_dev = target_feats.shape[0]
    block = jnp.concatenate(
        [
            source_feats,
            target_feats,
            log_b[None, :],
            jnp.pad(log_a, (0, feat - s_dev))[None, :],
            jnp.zeros((6, feat), jnp.float32),
        ],
        axis=0,
    )
    pieces = exchange(block, "src")
    sources, targets = n * s_dev, n * t_dev
    blk = 256
    f32, b16 = jnp.float32, jnp.bfloat16
    vmem = pl.BlockSpec(memory_space=pltpu.VMEM)
    f_pot, g_pot, src_moved, tgt_moved = pl.pallas_call(
        functools.partial(whole_group_kernel, n, s_dev, t_dev, blk),
        out_shape=[
            jax.ShapeDtypeStruct((s_dev, 1), f32),
            jax.ShapeDtypeStruct((1, t_dev), f32),
            jax.ShapeDtypeStruct((s_dev, feat), f32),
            jax.ShapeDtypeStruct((t_dev, feat), f32),
        ],
        in_specs=[vmem] * len(pieces),
        out_specs=[vmem] * 4,
        scratch_shapes=[
            pltpu.VMEM((sources, targets), f32),
            pltpu.VMEM((sources, 6 * feat), b16),
            pltpu.VMEM((targets, 6 * feat), b16),
            pltpu.VMEM((sources, 1), f32),
            pltpu.VMEM((sources, 1), f32),
            pltpu.VMEM((sources, 1), f32),
            pltpu.VMEM((s_dev, targets), f32),
            pltpu.VMEM((sources, t_dev), f32),
            pltpu.VMEM((8, targets), f32),
        ],
        compiler_params=pltpu.CompilerParams(vmem_limit_bytes=56 * 2**20),
        name="whole_group",
    )(*pieces)
    return f_pot.reshape(s_dev), g_pot.reshape(t_dev), src_moved, tgt_moved


def merged(part, axis, combine):
    gathered = jax.tree.map(lambda a: lax.all_gather(a, axis), part)

    def take(source):
        return jax.tree.map(lambda a: lax.dynamic_index_in_dim(a, source, 0, False), gathered)

    return lax.fori_loop(
        1, lax.axis_size(axis), lambda source, state: combine(state, take(source)), take(0)
    )


def pair_cost(rows, cols, rows_sq, cols_sq, width):
    inner = jnp.dot(rows, cols.T, precision=HI, preferred_element_type=jnp.float32)
    return (rows_sq[:, None] + cols_sq[None, :] - 2.0 * inner) / width


def row_update(cost, g_pot, log_mass):
    scores = (g_pot[None, :] - cost) / EPS
    top = jnp.max(scores, axis=1)
    total = jnp.sum(jnp.exp(scores - top[:, None]), axis=1)
    return EPS * log_mass - EPS * (top + jnp.log(total))


def combine_pairs(first, second):
    top = jnp.maximum(first[0], second[0])
    total = first[1] * jnp.exp(first[0] - top) + second[1] * jnp.exp(second[0] - top)
    return (top, total)


def per_device_rows(source_feats, target_feats, log_a, log_b):
    width = source_feats.shape[1]
    rows = target_feats.shape[0]
    tgt_all, log_b_all = (
        lax.all_gather(target_feats, "src", axis=0, tiled=True),
        lax.all_gather(log_b, "src", axis=0, tiled=True),
    )
    sq_src = jnp.sum(source_feats * source_feats, axis=1)
    sq_tgt = jnp.sum(tgt_all * tgt_all, axis=1)
    cost = pair_cost(source_feats, tgt_all, sq_src, sq_tgt, width)
    g_pot = jnp.zeros((tgt_all.shape[0],), jnp.float32)
    f_pot = jnp.zeros((source_feats.shape[0],), jnp.float32)
    for step in range(ITERS):
        f_pot = row_update(cost, g_pot, log_a)
        scores = (f_pot[:, None] - cost) / EPS
        local_top = jnp.max(scores, axis=0)
        local_total = jnp.sum(jnp.exp(scores - local_top[None, :]), axis=0)
        top, total = merged((local_top, local_total), "src", combine_pairs)
        g_pot = EPS * log_b_all - EPS * (top + jnp.log(total))
    plan = jnp.exp((f_pot[:, None] + g_pot[None, :] - cost) / EPS)
    carried = jnp.dot(plan, tgt_all, precision=HI, preferred_element_type=jnp.float32)
    src_moved = carried / jnp.sum(plan, axis=1)[:, None]
    own_start = lax.axis_index("src") * rows
    g_own = lax.dynamic_slice_in_dim(g_pot, own_start, rows)
    gathered = lax.psum_scatter(
        lax.dot_general(
            plan,
            source_feats,
            (((0,), (0,)), ((), ())),
            precision=HI,
            preferred_element_type=jnp.float32,
        ),
        "src",
        scatter_dimension=0,
        tiled=True,
    )
    tgt_moved = gathered / jnp.exp(log_b)[:, None]
    return (f_pot, g_own, src_moved, tgt_moved)


def per_device(source_feats, target_feats, log_a, log_b):
    n = lax.axis_size("src")
    s_dev, feat = source_feats.shape
    t_dev = target_feats.shape[0]
    fits = 4 * n * s_dev * n * t_dev <= REPLICATED_BYTES
    shaped = n >= 4 and n & (n - 1) == 0 and s_dev % 16 == 0 and s_dev <= feat == t_dev
    if fits and shaped and (n * s_dev) % 256 == 0:
        return per_device_whole(source_feats, target_feats, log_a, log_b)
    return per_device_rows(source_feats, target_feats, log_a, log_b)


def solution(mesh):
    both = P(("groups", "src"), None)
    line = P(("groups", "src"))
    return jax.shard_map(
        per_device,
        mesh=mesh,
        in_specs=(both, both, line, line),
        out_specs=(line, line, both, both),
        check_vma=False,
    )
```

```python
import functools

import jax
import jax.numpy as jnp
from jax import lax
from jax.experimental import pallas as pl
from jax.experimental.pallas import tpu as pltpu
from jax.sharding import PartitionSpec as P

ITERS = 3
EPS = 0.05
LN2 = 0.6931471805599453
LOG2E = 1.4426950408889634
SAFE = 2.0**30
WIDE = 2.0**60
PARTS = 8
REPLICATED_BYTES = 24 * 2**20
HI = lax.Precision.HIGHEST


def split3(a):
    first = a.astype(jnp.bfloat16)
    rest = a - first.astype(jnp.float32)
    second = rest.astype(jnp.bfloat16)
    third = (rest - second.astype(jnp.float32)).astype(jnp.bfloat16)
    return first, second, third


def nt_dot(a, b, precision=None):
    return lax.dot_general(
        a, b, (((1,), (1,)), ((), ())), precision=precision, preferred_element_type=jnp.float32
    )


def whole_group_kernel(n, s_dev, t_dev, blk, *refs):
    pieces = refs[:-14]
    f_ref, g_ref, sm_ref, tm_ref = refs[-14:-10]
    e_ref, xs, ys, la_col, u_col, rows_p, cols_p, acc, mb0, mb1 = refs[-10:]
    feat = pieces[0].shape[1]
    rows = s_dev + t_dev + 8
    k = LOG2E / (feat * EPS)
    sources, targets = n * s_dev, n * t_dev

    blocks = [(ref, at) for ref in pieces for at in range(0, ref.shape[0], rows)]
    center = sum(
        jnp.sum(ref[at + s_dev : at + s_dev + t_dev, :].reshape(t_dev // 8, 8, feat), axis=0)
        for ref, at in blocks
    )
    center = jnp.sum(center, axis=0, keepdims=True) * (1.0 / targets)
    las, lbs, norms = [], [], []
    ones = jnp.ones((8, 3 * feat), jnp.bfloat16)
    for d, (ref, at) in enumerate(blocks):
        x1, x2, x3 = split3((ref[at : at + s_dev, :] - center) * (2.0 * k))
        xs[d * s_dev : (d + 1) * s_dev, :] = jnp.concatenate([x1, x1, x2, x2, x1, x3], 1)
        y = ref[at + s_dev : at + s_dev + t_dev, :] - center
        y1, y2, y3 = split3(y)
        ys[d * t_dev : (d + 1) * t_dev, :] = jnp.concatenate([y1, y2, y1, y2, y3, y1], 1)
        norms.append(nt_dot(ones, jnp.concatenate(split3(y * y), 1))[0:1, :])
        lbs.append(ref[at + s_dev + t_dev : at + s_dev + t_dev + 1, :])
        las.append(ref[at + s_dev + t_dev + 1 : at + s_dev + t_dev + 2, :])
    norm = jnp.concatenate(norms, 1) * k
    shift = jnp.mean(norm, axis=1, keepdims=True)
    g1 = shift - norm
    mass_b = jnp.exp(jnp.concatenate(lbs, 1))
    la_t = jnp.exp(jnp.concatenate(las, 0)).T
    for d in range(n):
        la_col[d * s_dev : (d + 1) * s_dev, :] = la_t[:s_dev, d : d + 1]

    steps = sources // blk
    parts = PARTS
    chunk, sub = targets // parts, blk // parts

    def column_part(e, u):
        return jnp.sum((e * u).reshape(e.shape[0] // 8, 8, targets), axis=0)

    def product(dst, i, part):
        cols = slice(part * chunk, (part + 1) * chunk)
        dst[:, cols] = nt_dot(xs[i * blk : (i + 1) * blk, :], ys[cols, :])

    lows, highs = [], []

    def absorb(src, i, part):
        s = slice(i * blk + part * sub, i * blk + (part + 1) * sub)
        e = jnp.exp2(src[part * sub : (part + 1) * sub, :] + g1)
        e_ref[s, :] = e
        r = jnp.sum(e, axis=1, keepdims=True)
        lows.append(jnp.min(r))
        highs.append(jnp.max(r))
        acc[...] += column_part(e, la_col[s, :] / r)

    def column_end():
        total = jnp.sum(acc[...], axis=0, keepdims=True)
        lows.append(jnp.min(total))
        highs.append(jnp.max(total) * (WIDE / SAFE))
        return total

    acc[...] = jnp.zeros_like(acc)
    bufs = (mb0, mb1)
    for part in range(parts):
        product(bufs[0], 0, part)
    for i in range(steps):
        for part in range(parts):
            if i + 1 < steps:
                product(bufs[(i + 1) % 2], i + 1, part)
            absorb(bufs[i % 2], i, part)
    total = column_end()

    for _ in range(1, ITERS):
        v = mass_b / total
        acc[...] = jnp.zeros_like(acc)
        for i in range(steps):
            s = slice(i * blk, (i + 1) * blk)
            e = e_ref[s, :]
            r = jnp.sum(e * v, axis=1, keepdims=True)
            lows.append(jnp.min(r))
            highs.append(jnp.max(r))
            u = la_col[s, :] / r
            u_col[s, :] = u
            acc[...] += column_part(e, u)
        total = column_end()
    v = mass_b / total
    safe = (functools.reduce(jnp.minimum, lows) > 1.0 / SAFE) & (
        functools.reduce(jnp.maximum, highs) < WIDE
    )

    x_own = pieces[0][0:s_dev, :] - center
    sq_own = k * jnp.sum(x_own * x_own, axis=1, keepdims=True)

    def put_f(f):
        wide = jnp.broadcast_to(f, (s_dev, feat))
        wide = jnp.concatenate([wide, jnp.zeros((feat - s_dev, feat), jnp.float32)], 0)
        f_ref[...] = wide.T[0:1, 0:s_dev]

    @pl.when(safe)
    def _():
        put_f(EPS * jnp.log(u_col[0:s_dev, :]) + (EPS * LN2) * (sq_own + shift))
        g_ref[...] = EPS * jnp.log(v[:, 0:t_dev])
        rows_p[...] = e_ref[0:s_dev, :] * v
        cols_p[...] = e_ref[:, 0:t_dev] * u_col[...] * (1.0 / total[:, 0:t_dev])

    @pl.when(jnp.logical_not(safe))
    def _():
        log_b = jnp.log2(mass_b)

        def at_block(i):
            return pl.ds(pl.multiple_of(i * blk, blk), blk)

        def inner(i, carry):
            s = at_block(i)
            e_ref[s, :] = nt_dot(xs[s, :], ys[...])
            return carry

        lax.fori_loop(0, steps, inner, 0)

        def potentials(step, g):
            def row(i, carry):
                s = at_block(i)
                t = e_ref[s, :] + g
                top = jnp.max(t, axis=1, keepdims=True)
                total = jnp.sum(jnp.exp2(t - top), axis=1, keepdims=True)
                u_col[s, :] = jnp.log2(la_col[s, :]) - top - jnp.log2(total)
                return carry

            lax.fori_loop(0, steps, row, 0)

            def column_top(i, top):
                s = at_block(i)
                return jnp.maximum(top, jnp.max(e_ref[s, :] + u_col[s, :], axis=0, keepdims=True))

            top = lax.fori_loop(0, steps, column_top, jnp.full((1, targets), -jnp.inf, jnp.float32))

            def column_total(i, total):
                s = at_block(i)
                e = jnp.exp2(e_ref[s, :] + u_col[s, :] - top)
                return total + jnp.sum(e, axis=0, keepdims=True)

            total = lax.fori_loop(0, steps, column_total, jnp.zeros((1, targets), jnp.float32))
            return log_b - top - jnp.log2(total)

        g = lax.fori_loop(0, ITERS, potentials, -norm)
        put_f((EPS * LN2) * (u_col[0:s_dev, :] + sq_own))
        g_ref[...] = (EPS * LN2) * (g[:, 0:t_dev] + norm[:, 0:t_dev])
        rows_p[...] = jnp.exp2(e_ref[0:s_dev, :] + u_col[0:s_dev, :] + g)
        own = jnp.exp2(e_ref[:, 0:t_dev] + u_col[...] + g[:, 0:t_dev])
        cols_p[...] = own * (1.0 / mass_b[:, 0:t_dev])

    plan_rows = rows_p[...]
    mass = jnp.sum(plan_rows, axis=1, keepdims=True)
    p1, p2, _ = split3(plan_rows)
    y1, y2 = ys[:, 0:feat], ys[:, feat : 2 * feat]

    def nn(a, b):
        return jnp.dot(a, b, preferred_element_type=jnp.float32)

    sm_ref[...] = (nn(p1, y1) + (nn(p1, y2) + nn(p2, y1))) / mass + center

    def tn(a, b):
        return lax.dot_general(a, b, (((0,), (0,)), ((), ())), preferred_element_type=jnp.float32)

    q1, q2, _ = split3(cols_p[...])
    x1, x2 = xs[:, 0:feat], xs[:, 2 * feat : 3 * feat]
    tm_ref[...] = (tn(q1, x1) + (tn(q1, x2) + tn(q2, x1))) * (1.0 / (2.0 * k)) + center


def exchange(block, axis):
    n = lax.axis_size(axis)

    def swap(a, bits):
        return lax.ppermute(a, axis, [(i, i ^ bits) for i in range(n)])

    far = [swap(block, bits) for bits in range(4, n, 4)]
    line = [block] + far
    side = [swap(a, 2) for a in line]
    mine = jnp.concatenate(line + side, axis=0)
    return [mine, swap(mine, 1)]


def per_device_whole(source_feats, target_feats, log_a, log_b):
    n = lax.axis_size("src")
    s_dev, feat = source_feats.shape
    t_dev = target_feats.shape[0]
    block = jnp.concatenate(
        [
            source_feats,
            target_feats,
            log_b[None, :],
            jnp.pad(log_a, (0, feat - s_dev))[None, :],
            jnp.zeros((6, feat), jnp.float32),
        ],
        axis=0,
    )
    pieces = exchange(block, "src")
    sources, targets = n * s_dev, n * t_dev
    blk = 256
    f32, b16 = jnp.float32, jnp.bfloat16
    vmem = pl.BlockSpec(memory_space=pltpu.VMEM)
    f_pot, g_pot, src_moved, tgt_moved = pl.pallas_call(
        functools.partial(whole_group_kernel, n, s_dev, t_dev, blk),
        out_shape=[
            jax.ShapeDtypeStruct((1, s_dev), f32),
            jax.ShapeDtypeStruct((1, t_dev), f32),
            jax.ShapeDtypeStruct((s_dev, feat), f32),
            jax.ShapeDtypeStruct((t_dev, feat), f32),
        ],
        in_specs=[vmem] * len(pieces),
        out_specs=[vmem] * 4,
        scratch_shapes=[
            pltpu.VMEM((sources, targets), f32),
            pltpu.VMEM((sources, 6 * feat), b16),
            pltpu.VMEM((targets, 6 * feat), b16),
            pltpu.VMEM((sources, 1), f32),
            pltpu.VMEM((sources, 1), f32),
            pltpu.VMEM((s_dev, targets), f32),
            pltpu.VMEM((sources, t_dev), f32),
            pltpu.VMEM((8, targets), f32),
            pltpu.VMEM((blk, targets), f32),
            pltpu.VMEM((blk, targets), f32),
        ],
        compiler_params=pltpu.CompilerParams(vmem_limit_bytes=36 * 2**20),
        name="whole_group",
    )(*pieces)
    return f_pot.reshape(s_dev), g_pot.reshape(t_dev), src_moved, tgt_moved


def merged(part, axis, combine):
    gathered = jax.tree.map(lambda a: lax.all_gather(a, axis), part)

    def take(source):
        return jax.tree.map(lambda a: lax.dynamic_index_in_dim(a, source, 0, False), gathered)

    return lax.fori_loop(
        1, lax.axis_size(axis), lambda source, state: combine(state, take(source)), take(0)
    )


def pair_cost(rows, cols, rows_sq, cols_sq, width):
    inner = jnp.dot(rows, cols.T, precision=HI, preferred_element_type=jnp.float32)
    return (rows_sq[:, None] + cols_sq[None, :] - 2.0 * inner) / width


def row_update(cost, g_pot, log_mass):
    scores = (g_pot[None, :] - cost) / EPS
    top = jnp.max(scores, axis=1)
    total = jnp.sum(jnp.exp(scores - top[:, None]), axis=1)
    return EPS * log_mass - EPS * (top + jnp.log(total))


def combine_pairs(first, second):
    top = jnp.maximum(first[0], second[0])
    total = first[1] * jnp.exp(first[0] - top) + second[1] * jnp.exp(second[0] - top)
    return (top, total)


def per_device_rows(source_feats, target_feats, log_a, log_b):
    width = source_feats.shape[1]
    rows = target_feats.shape[0]
    tgt_all, log_b_all = (
        lax.all_gather(target_feats, "src", axis=0, tiled=True),
        lax.all_gather(log_b, "src", axis=0, tiled=True),
    )
    sq_src = jnp.sum(source_feats * source_feats, axis=1)
    sq_tgt = jnp.sum(tgt_all * tgt_all, axis=1)
    cost = pair_cost(source_feats, tgt_all, sq_src, sq_tgt, width)
    g_pot = jnp.zeros((tgt_all.shape[0],), jnp.float32)
    f_pot = jnp.zeros((source_feats.shape[0],), jnp.float32)
    for step in range(ITERS):
        f_pot = row_update(cost, g_pot, log_a)
        scores = (f_pot[:, None] - cost) / EPS
        local_top = jnp.max(scores, axis=0)
        local_total = jnp.sum(jnp.exp(scores - local_top[None, :]), axis=0)
        top, total = merged((local_top, local_total), "src", combine_pairs)
        g_pot = EPS * log_b_all - EPS * (top + jnp.log(total))
    plan = jnp.exp((f_pot[:, None] + g_pot[None, :] - cost) / EPS)
    carried = jnp.dot(plan, tgt_all, precision=HI, preferred_element_type=jnp.float32)
    src_moved = carried / jnp.sum(plan, axis=1)[:, None]
    own_start = lax.axis_index("src") * rows
    g_own = lax.dynamic_slice_in_dim(g_pot, own_start, rows)
    gathered = lax.psum_scatter(
        lax.dot_general(
            plan,
            source_feats,
            (((0,), (0,)), ((), ())),
            precision=HI,
            preferred_element_type=jnp.float32,
        ),
        "src",
        scatter_dimension=0,
        tiled=True,
    )
    tgt_moved = gathered / jnp.exp(log_b)[:, None]
    return (f_pot, g_own, src_moved, tgt_moved)


def per_device(source_feats, target_feats, log_a, log_b):
    n = lax.axis_size("src")
    s_dev, feat = source_feats.shape
    t_dev = target_feats.shape[0]
    fits = 4 * n * s_dev * n * t_dev <= REPLICATED_BYTES
    shaped = n >= 4 and n & (n - 1) == 0 and s_dev % 16 == 0 and s_dev <= feat == t_dev
    if fits and shaped and (n * s_dev) % 256 == 0:
        return per_device_whole(source_feats, target_feats, log_a, log_b)
    return per_device_rows(source_feats, target_feats, log_a, log_b)


def solution(mesh):
    both = P(("groups", "src"), None)
    line = P(("groups", "src"))
    return jax.shard_map(
        per_device,
        mesh=mesh,
        in_specs=(both, both, line, line),
        out_specs=(line, line, both, both),
        check_vma=False,
    )
```

```python
import functools

import jax
import jax.numpy as jnp
from jax import lax
from jax.experimental import pallas as pl
from jax.experimental.pallas import tpu as pltpu
from jax.sharding import PartitionSpec as P

ITERS = 3
EPS = 0.05
LN2 = 0.6931471805599453
LOG2E = 1.4426950408889634
SAFE = 2.0**30
WIDE = 2.0**60
PARTS = 8
REPLICATED_BYTES = 24 * 2**20
HI = lax.Precision.HIGHEST


def split3(a):
    first = a.astype(jnp.bfloat16)
    rest = a - first.astype(jnp.float32)
    second = rest.astype(jnp.bfloat16)
    third = (rest - second.astype(jnp.float32)).astype(jnp.bfloat16)
    return first, second, third


def split2(a):
    first = a.astype(jnp.bfloat16)
    return first, (a - first.astype(jnp.float32)).astype(jnp.bfloat16)


def nt_dot(a, b, precision=None):
    return lax.dot_general(
        a, b, (((1,), (1,)), ((), ())), precision=precision, preferred_element_type=jnp.float32
    )


def whole_group_kernel(n, s_dev, t_dev, blk, *refs):
    pieces = refs[:-14]
    f_ref, g_ref, sm_ref, tm_ref = refs[-14:-10]
    e_ref, xs, ys, la_col, u_col, rows_p, cols_p, acc, mb0, mb1 = refs[-10:]
    feat = pieces[0].shape[1]
    rows = s_dev + t_dev + 8
    k = LOG2E / (feat * EPS)
    sources, targets = n * s_dev, n * t_dev

    blocks = [(ref, at) for ref in pieces for at in range(0, ref.shape[0], rows)]
    center = sum(
        jnp.sum(ref[at + s_dev : at + s_dev + t_dev, :].reshape(t_dev // 8, 8, feat), axis=0)
        for ref, at in blocks
    )
    center = jnp.sum(center, axis=0, keepdims=True) * (1.0 / targets)
    las, lbs, norms = [], [], []
    ones = jnp.ones((8, 3 * feat), jnp.bfloat16)
    for d, (ref, at) in enumerate(blocks):
        x1, x2 = split2((ref[at : at + s_dev, :] - center) * (2.0 * k))
        xs[d * s_dev : (d + 1) * s_dev, :] = jnp.concatenate([x1, x1, x2, x2], 1)
        y = ref[at + s_dev : at + s_dev + t_dev, :] - center
        y1, y2 = split2(y)
        ys[d * t_dev : (d + 1) * t_dev, :] = jnp.concatenate([y1, y2, y1, y2], 1)
        norms.append(nt_dot(ones, jnp.concatenate(split3(y * y), 1))[0:1, :])
        lbs.append(ref[at + s_dev + t_dev : at + s_dev + t_dev + 1, :])
        las.append(ref[at + s_dev + t_dev + 1 : at + s_dev + t_dev + 2, :])
    norm = jnp.concatenate(norms, 1) * k
    shift = jnp.mean(norm, axis=1, keepdims=True)
    g1 = shift - norm
    mass_b = jnp.exp(jnp.concatenate(lbs, 1))
    la_t = jnp.exp(jnp.concatenate(las, 0)).T
    for d in range(n):
        la_col[d * s_dev : (d + 1) * s_dev, :] = la_t[:s_dev, d : d + 1]

    steps = sources // blk
    parts = PARTS
    chunk, sub = targets // parts, blk // parts

    def least(values):
        return functools.reduce(jnp.minimum, values)

    def most(values):
        return functools.reduce(jnp.maximum, values)

    def column_part(e, u):
        return jnp.sum((e * u).reshape(e.shape[0] // 8, 8, targets), axis=0)

    def product(dst, i, part):
        cols = slice(part * chunk, (part + 1) * chunk)
        dst[:, cols] = nt_dot(xs[i * blk : (i + 1) * blk, :], ys[cols, :])

    sums, ends = [], []

    def absorb(src, i, part):
        s = slice(i * blk + part * sub, i * blk + (part + 1) * sub)
        e = jnp.exp2(src[part * sub : (part + 1) * sub, :] + g1)
        e_ref[s, :] = e
        r = jnp.sum(e, axis=1, keepdims=True)
        sums.append(r)
        acc[...] += column_part(e, la_col[s, :] / r)

    def column_end():
        total = jnp.sum(acc[...], axis=0, keepdims=True)
        ends.append(total)
        return total

    acc[...] = jnp.zeros_like(acc)
    bufs = (mb0, mb1)
    for part in range(parts):
        product(bufs[0], 0, part)
    for i in range(steps):
        for part in range(parts):
            if i + 1 < steps:
                product(bufs[(i + 1) % 2], i + 1, part)
            absorb(bufs[i % 2], i, part)
    total = column_end()

    for _ in range(1, ITERS):
        v = mass_b / total
        acc[...] = jnp.zeros_like(acc)
        for i in range(steps):
            s = slice(i * blk, (i + 1) * blk)
            e = e_ref[s, :]
            r = jnp.sum(e * v, axis=1, keepdims=True)
            sums.extend(r[p * sub : (p + 1) * sub, :] for p in range(parts))
            u = la_col[s, :] / r
            u_col[s, :] = u
            acc[...] += column_part(e, u)
        total = column_end()
    v = mass_b / total
    low = jnp.minimum(jnp.min(least(sums)), jnp.min(least(ends)))
    high = jnp.maximum(jnp.max(most(sums)), jnp.max(most(ends)) * (WIDE / SAFE))
    safe = (low > 1.0 / SAFE) & (high < WIDE)

    x_own = pieces[0][0:s_dev, :] - center
    sq_own = k * jnp.sum(x_own * x_own, axis=1, keepdims=True)

    def put_f(f):
        wide = jnp.broadcast_to(f, (s_dev, feat))
        wide = jnp.concatenate([wide, jnp.zeros((feat - s_dev, feat), jnp.float32)], 0)
        f_ref[...] = wide.T[0:1, 0:s_dev]

    @pl.when(safe)
    def _():
        put_f(EPS * jnp.log(u_col[0:s_dev, :]) + (EPS * LN2) * (sq_own + shift))
        g_ref[...] = EPS * jnp.log(v[:, 0:t_dev])
        rows_p[...] = e_ref[0:s_dev, :] * v
        cols_p[...] = e_ref[:, 0:t_dev] * u_col[...] * (1.0 / total[:, 0:t_dev])

    @pl.when(jnp.logical_not(safe))
    def _():
        log_b = jnp.log2(mass_b)

        def at_block(i):
            return pl.ds(pl.multiple_of(i * blk, blk), blk)

        def inner(i, carry):
            s = at_block(i)
            e_ref[s, :] = nt_dot(xs[s, :], ys[...])
            return carry

        lax.fori_loop(0, steps, inner, 0)

        def potentials(step, g):
            def row(i, carry):
                s = at_block(i)
                t = e_ref[s, :] + g
                top = jnp.max(t, axis=1, keepdims=True)
                total = jnp.sum(jnp.exp2(t - top), axis=1, keepdims=True)
                u_col[s, :] = jnp.log2(la_col[s, :]) - top - jnp.log2(total)
                return carry

            lax.fori_loop(0, steps, row, 0)

            def column_top(i, top):
                s = at_block(i)
                return jnp.maximum(top, jnp.max(e_ref[s, :] + u_col[s, :], axis=0, keepdims=True))

            top = lax.fori_loop(0, steps, column_top, jnp.full((1, targets), -jnp.inf, jnp.float32))

            def column_total(i, total):
                s = at_block(i)
                e = jnp.exp2(e_ref[s, :] + u_col[s, :] - top)
                return total + jnp.sum(e, axis=0, keepdims=True)

            total = lax.fori_loop(0, steps, column_total, jnp.zeros((1, targets), jnp.float32))
            return log_b - top - jnp.log2(total)

        g = lax.fori_loop(0, ITERS, potentials, -norm)
        put_f((EPS * LN2) * (u_col[0:s_dev, :] + sq_own))
        g_ref[...] = (EPS * LN2) * (g[:, 0:t_dev] + norm[:, 0:t_dev])
        rows_p[...] = jnp.exp2(e_ref[0:s_dev, :] + u_col[0:s_dev, :] + g)
        own = jnp.exp2(e_ref[:, 0:t_dev] + u_col[...] + g[:, 0:t_dev])
        cols_p[...] = own * (1.0 / mass_b[:, 0:t_dev])

    plan_rows = rows_p[...]
    mass = jnp.sum(plan_rows, axis=1, keepdims=True)
    p1, p2 = split2(plan_rows)
    y1, y2 = ys[:, 0:feat], ys[:, feat : 2 * feat]

    def nn(a, b):
        return jnp.dot(a, b, preferred_element_type=jnp.float32)

    sm_ref[...] = (nn(p1, y1) + (nn(p1, y2) + nn(p2, y1))) / mass + center

    def tn(a, b):
        return lax.dot_general(a, b, (((0,), (0,)), ((), ())), preferred_element_type=jnp.float32)

    q1, q2 = split2(cols_p[...])
    x1, x2 = xs[:, 0:feat], xs[:, 2 * feat : 3 * feat]
    tm_ref[...] = (tn(q1, x1) + (tn(q1, x2) + tn(q2, x1))) * (1.0 / (2.0 * k)) + center


def exchange(block, axis):
    n = lax.axis_size(axis)

    def swap(a, bits):
        return lax.ppermute(a, axis, [(i, i ^ bits) for i in range(n)])

    step = [swap(block, 4)]
    for bits in range(8, n, 8):
        jump = swap(block, bits)
        step += [jump, swap(jump, 4)]
    line = jnp.concatenate([block] + step, axis=0)
    side = jnp.concatenate([swap(a, 2) for a in [block] + step], axis=0)
    return [line, swap(line, 1), side, swap(side, 1)]


def pack_kernel(x_ref, y_ref, la_ref, lb_ref, out_ref, la_row, lb_row, sems):
    s_dev, t_dev = x_ref.shape[0], y_ref.shape[0]
    rows = s_dev + t_dev
    copies = [
        pltpu.make_async_copy(src, dst, sems.at[i])
        for i, (src, dst) in enumerate(
            (
                (x_ref, out_ref.at[0:s_dev, :]),
                (y_ref, out_ref.at[s_dev:rows, :]),
                (la_ref, la_row),
                (lb_ref, lb_row),
            )
        )
    ]
    for copy in copies:
        copy.start()
    out_ref[rows:, :] = jnp.zeros((8, x_ref.shape[1]), jnp.float32)
    copies[2].wait()
    out_ref[rows + 1 : rows + 2, 0:s_dev] = la_row[...].reshape(1, s_dev)
    copies[3].wait()
    out_ref[rows : rows + 1, :] = lb_row[...].reshape(1, t_dev)
    copies[0].wait()
    copies[1].wait()


def per_device_whole(source_feats, target_feats, log_a, log_b):
    n = lax.axis_size("src")
    s_dev, feat = source_feats.shape
    t_dev = target_feats.shape[0]
    block = pl.pallas_call(
        pack_kernel,
        out_shape=jax.ShapeDtypeStruct((s_dev + t_dev + 8, feat), jnp.float32),
        in_specs=[pl.BlockSpec(memory_space=pltpu.HBM)] * 4,
        out_specs=pl.BlockSpec(memory_space=pltpu.VMEM),
        scratch_shapes=[
            pltpu.VMEM((s_dev,), jnp.float32),
            pltpu.VMEM((t_dev,), jnp.float32),
            pltpu.SemaphoreType.DMA((4,)),
        ],
        compiler_params=pltpu.CompilerParams(vmem_limit_bytes=60 * 2**20),
        name="pack",
    )(source_feats, target_feats, log_a, log_b)
    pieces = exchange(block, "src")
    sources, targets = n * s_dev, n * t_dev
    blk = 256
    f32, b16 = jnp.float32, jnp.bfloat16
    vmem = pl.BlockSpec(memory_space=pltpu.VMEM)
    f_pot, g_pot, src_moved, tgt_moved = pl.pallas_call(
        functools.partial(whole_group_kernel, n, s_dev, t_dev, blk),
        out_shape=[
            jax.ShapeDtypeStruct((1, s_dev), f32),
            jax.ShapeDtypeStruct((1, t_dev), f32),
            jax.ShapeDtypeStruct((s_dev, feat), f32),
            jax.ShapeDtypeStruct((t_dev, feat), f32),
        ],
        in_specs=[vmem] * len(pieces),
        out_specs=[vmem] * 4,
        scratch_shapes=[
            pltpu.VMEM((sources, targets), f32),
            pltpu.VMEM((sources, 4 * feat), b16),
            pltpu.VMEM((targets, 4 * feat), b16),
            pltpu.VMEM((sources, 1), f32),
            pltpu.VMEM((sources, 1), f32),
            pltpu.VMEM((s_dev, targets), f32),
            pltpu.VMEM((sources, t_dev), f32),
            pltpu.VMEM((8, targets), f32),
            pltpu.VMEM((blk, targets), f32),
            pltpu.VMEM((blk, targets), f32),
        ],
        compiler_params=pltpu.CompilerParams(vmem_limit_bytes=36 * 2**20),
        name="whole_group",
    )(*pieces)
    return f_pot.reshape(s_dev), g_pot.reshape(t_dev), src_moved, tgt_moved


def merged(part, axis, combine):
    gathered = jax.tree.map(lambda a: lax.all_gather(a, axis), part)

    def take(source):
        return jax.tree.map(lambda a: lax.dynamic_index_in_dim(a, source, 0, False), gathered)

    return lax.fori_loop(
        1, lax.axis_size(axis), lambda source, state: combine(state, take(source)), take(0)
    )


def pair_cost(rows, cols, rows_sq, cols_sq, width):
    inner = jnp.dot(rows, cols.T, precision=HI, preferred_element_type=jnp.float32)
    return (rows_sq[:, None] + cols_sq[None, :] - 2.0 * inner) / width


def row_update(cost, g_pot, log_mass):
    scores = (g_pot[None, :] - cost) / EPS
    top = jnp.max(scores, axis=1)
    total = jnp.sum(jnp.exp(scores - top[:, None]), axis=1)
    return EPS * log_mass - EPS * (top + jnp.log(total))


def combine_pairs(first, second):
    top = jnp.maximum(first[0], second[0])
    total = first[1] * jnp.exp(first[0] - top) + second[1] * jnp.exp(second[0] - top)
    return (top, total)


def per_device_rows(source_feats, target_feats, log_a, log_b):
    width = source_feats.shape[1]
    rows = target_feats.shape[0]
    tgt_all, log_b_all = (
        lax.all_gather(target_feats, "src", axis=0, tiled=True),
        lax.all_gather(log_b, "src", axis=0, tiled=True),
    )
    sq_src = jnp.sum(source_feats * source_feats, axis=1)
    sq_tgt = jnp.sum(tgt_all * tgt_all, axis=1)
    cost = pair_cost(source_feats, tgt_all, sq_src, sq_tgt, width)
    g_pot = jnp.zeros((tgt_all.shape[0],), jnp.float32)
    f_pot = jnp.zeros((source_feats.shape[0],), jnp.float32)
    for step in range(ITERS):
        f_pot = row_update(cost, g_pot, log_a)
        scores = (f_pot[:, None] - cost) / EPS
        local_top = jnp.max(scores, axis=0)
        local_total = jnp.sum(jnp.exp(scores - local_top[None, :]), axis=0)
        top, total = merged((local_top, local_total), "src", combine_pairs)
        g_pot = EPS * log_b_all - EPS * (top + jnp.log(total))
    plan = jnp.exp((f_pot[:, None] + g_pot[None, :] - cost) / EPS)
    carried = jnp.dot(plan, tgt_all, precision=HI, preferred_element_type=jnp.float32)
    src_moved = carried / jnp.sum(plan, axis=1)[:, None]
    own_start = lax.axis_index("src") * rows
    g_own = lax.dynamic_slice_in_dim(g_pot, own_start, rows)
    gathered = lax.psum_scatter(
        lax.dot_general(
            plan,
            source_feats,
            (((0,), (0,)), ((), ())),
            precision=HI,
            preferred_element_type=jnp.float32,
        ),
        "src",
        scatter_dimension=0,
        tiled=True,
    )
    tgt_moved = gathered / jnp.exp(log_b)[:, None]
    return (f_pot, g_own, src_moved, tgt_moved)


def per_device(source_feats, target_feats, log_a, log_b):
    n = lax.axis_size("src")
    s_dev, feat = source_feats.shape
    t_dev = target_feats.shape[0]
    fits = 4 * n * s_dev * n * t_dev <= REPLICATED_BYTES
    shaped = n >= 4 and n & (n - 1) == 0 and s_dev % 16 == 0 and s_dev <= feat == t_dev
    if fits and shaped and (n * s_dev) % 256 == 0:
        return per_device_whole(source_feats, target_feats, log_a, log_b)
    return per_device_rows(source_feats, target_feats, log_a, log_b)


def solution(mesh):
    both = P(("groups", "src"), None)
    line = P(("groups", "src"))
    return jax.shard_map(
        per_device,
        mesh=mesh,
        in_specs=(both, both, line, line),
        out_specs=(line, line, both, both),
        check_vma=False,
    )
```

```python
import functools

import jax
import jax.numpy as jnp
from jax import lax
from jax.experimental import pallas as pl
from jax.experimental.pallas import tpu as pltpu
from jax.sharding import PartitionSpec as P

ITERS = 3
EPS = 0.05
LN2 = 0.6931471805599453
LOG2E = 1.4426950408889634
SAFE = 2.0**30
WIDE = 2.0**60
PARTS = 8
CHUNK = 256
NEAR_VMEM = 16 * 2**20
WHOLE_VMEM = 36 * 2**20
REPLICATED_BYTES = 24 * 2**20
HI = lax.Precision.HIGHEST


def split3(a):
    first = a.astype(jnp.bfloat16)
    rest = a - first.astype(jnp.float32)
    second = rest.astype(jnp.bfloat16)
    third = (rest - second.astype(jnp.float32)).astype(jnp.bfloat16)
    return first, second, third


def split2(a):
    first = a.astype(jnp.bfloat16)
    return first, (a - first.astype(jnp.float32)).astype(jnp.bfloat16)


def nt_dot(a, b, precision=None):
    return lax.dot_general(
        a, b, (((1,), (1,)), ((), ())), precision=precision, preferred_element_type=jnp.float32
    )


def least(values):
    return functools.reduce(jnp.minimum, values)


def most(values):
    return functools.reduce(jnp.maximum, values)


def blocks_of(pieces, rows):
    return [(ref, at) for ref in pieces for at in range(0, ref.shape[0], rows)]


def target_sum(blocks, s_dev, t_dev):
    total = sum(
        jnp.sum(ref[at + s_dev : at + s_dev + t_dev, :].reshape(t_dev // 8, 8, -1), axis=0)
        for ref, at in blocks
    )
    return jnp.sum(total, axis=0, keepdims=True)


def split_features(blocks, s_dev, t_dev, center, k, xs, ys):
    feat = center.shape[1]
    norms = []
    ones = jnp.ones((8, 3 * feat), jnp.bfloat16)
    for d, (ref, at) in enumerate(blocks):
        x1, x2 = split2((ref[at : at + s_dev, :] - center) * (2.0 * k))
        xs[d * s_dev : (d + 1) * s_dev, :] = jnp.concatenate([x1, x1, x2, x2], 1)
        y = ref[at + s_dev : at + s_dev + t_dev, :] - center
        y1, y2 = split2(y)
        ys[d * t_dev : (d + 1) * t_dev, :] = jnp.concatenate([y1, y2, y1, y2], 1)
        norms.append(nt_dot(ones, jnp.concatenate(split3(y * y), 1))[0:1, :])
    return jnp.concatenate(norms, 1) * k


def near_kernel(s_dev, t_dev, blk, *refs):
    pieces = refs[:-8]
    e_ref, xs, ys, r_ref, norm_ref, mid_ref, mb0, mb1 = refs[-8:]
    feat = pieces[0].shape[1]
    k = LOG2E / (feat * EPS)
    blocks = blocks_of(pieces, s_dev + t_dev + 8)
    sources, targets = len(blocks) * s_dev, len(blocks) * t_dev
    center = target_sum(blocks, s_dev, t_dev) * (1.0 / targets)
    norm = split_features(blocks, s_dev, t_dev, center, k, xs, ys)
    norm_ref[...] = norm
    shift = jnp.mean(norm, axis=1, keepdims=True)
    mid_ref[0:1, :] = center
    mid_ref[1:2, :] = jnp.broadcast_to(shift, (1, feat))
    mid_ref[2:8, :] = jnp.zeros((6, feat), jnp.float32)
    g1 = shift - norm
    bufs = (mb0, mb1)
    steps = sources // blk
    bufs[0][...] = nt_dot(xs[0:blk, :], ys[...])
    for i in range(steps):
        if i + 1 < steps:
            bufs[(i + 1) % 2][...] = nt_dot(xs[(i + 1) * blk : (i + 2) * blk, :], ys[...])
        s = slice(i * blk, (i + 1) * blk)
        e = jnp.exp2(bufs[i % 2][...] + g1)
        e_ref[s, :] = e
        r_ref[s, :] = jnp.sum(e, axis=1, keepdims=True)


def whole_group_kernel(n, s_dev, t_dev, blk, *refs):
    pieces = refs[:-22]
    e11, xs1, ys1, r1_ref, norm_ref, mid_ref = refs[-22:-16]
    f_ref, g_ref, sm_ref, tm_ref = refs[-16:-12]
    e12, e21, e22, e_own, xs2, ys2, la_col, u_col, acc0, acc1, mb0, mb1 = refs[-12:]
    feat = pieces[0].shape[1]
    rows = s_dev + t_dev + 8
    k = LOG2E / (feat * EPS)
    sources, targets = n * s_dev, n * t_dev
    half_s, half_t = sources // 2, targets // 2
    xs, ys, accs = (xs1, xs2), (ys1, ys2), (acc0, acc1)

    blocks = blocks_of(pieces, rows)
    center = mid_ref[0:1, :]
    shift = mid_ref[1:2, 0:1]
    norms = (norm_ref[...], split_features(blocks[n // 2 :], s_dev, t_dev, center, k, xs2, ys2))
    lbs = [ref[at + s_dev + t_dev : at + s_dev + t_dev + 1, :] for ref, at in blocks]
    las = [ref[at + s_dev + t_dev + 1 : at + s_dev + t_dev + 2, :] for ref, at in blocks]
    g1 = tuple(shift - norm for norm in norms)
    mass_b = tuple(jnp.exp(jnp.concatenate(part, 1)) for part in (lbs[: n // 2], lbs[n // 2 :]))
    la_t = jnp.exp(jnp.concatenate(las, 0)).T
    for d in range(n):
        la_col[d * s_dev : (d + 1) * s_dev, :] = la_t[:s_dev, d : d + 1]

    steps = sources // blk
    near = steps // 2
    parts = PARTS
    sub = blk // parts

    def halves(i, first=e11):
        at = (i % near) * blk
        return ((first, e12) if i < near else (e21, e22)), slice(at, at + blk)

    def column_part(e, u):
        return jnp.sum((e * u).reshape(e.shape[0] // 8, 8, half_t), axis=0)

    def product(dst, i, part):
        at = (i % near) * blk
        factor = xs[i // near][at : at + blk, :]
        chunks = [
            (h, slice(c, c + CHUNK))
            for h in ((1,) if i < near else (0, 1))
            for c in range(0, half_t, CHUNK)
        ]
        for h, cols in chunks[part * len(chunks) // parts : (part + 1) * len(chunks) // parts]:
            dst[:, h * half_t + cols.start : h * half_t + cols.stop] = nt_dot(factor, ys[h][cols, :])

    sums, ends = [], []

    def absorb(src, i, part):
        kept, where = halves(i)
        local = slice(part * sub, (part + 1) * sub)
        s = slice(where.start + local.start, where.start + local.stop)
        e1 = jnp.exp2(src[local, half_t:] + g1[1])
        kept[1][s, :] = e1
        if i < near:
            e0 = kept[0][s, :]
            r = r1_ref[s, :] + jnp.sum(e1, axis=1, keepdims=True)
        else:
            e0 = jnp.exp2(src[local, :half_t] + g1[0])
            kept[0][s, :] = e0
            r = jnp.sum(e0 + e1, axis=1, keepdims=True)
        sums.append(r)
        u = la_col[i * blk + local.start : i * blk + local.stop, :] / r
        acc0[...] += column_part(e0, u)
        acc1[...] += column_part(e1, u)

    def column_end():
        total = tuple(jnp.sum(acc[...], axis=0, keepdims=True) for acc in accs)
        ends.extend(total)
        return total

    def clear():
        for acc in accs:
            acc[...] = jnp.zeros_like(acc)

    clear()
    bufs = (mb0, mb1)
    for part in range(parts):
        product(bufs[0], 0, part)
    for i in range(steps):
        for part in range(parts):
            if i + 1 < steps:
                product(bufs[(i + 1) % 2], i + 1, part)
            absorb(bufs[i % 2], i, part)
    total = column_end()

    def quarters_sum(wide, count):
        low = wide[:count, feat:] + (wide[count:, :feat] + wide[count:, feat:])
        return wide[:count, :feat] + low

    def target_sums(plan, i):
        at = (i % near) * blk
        return lax.dot_general(
            jnp.concatenate(split2(plan), 1),
            xs[i // near][at : at + blk, feat : 3 * feat],
            (((0,), (0,)), ((), ())),
            preferred_element_type=jnp.float32,
        )

    def put_targets(sums_of, mass):
        moved = quarters_sum(sum(sums_of), t_dev)
        mass = jnp.broadcast_to(mass * (2.0 * k), (feat, t_dev)).T
        tm_ref[...] = moved / mass + center

    def put_sources(plan):
        mass = jnp.sum(plan[0] + plan[1], axis=1, keepdims=True)
        wide = sum(
            jnp.dot(
                jnp.concatenate(split2(plan[h]), 0),
                ys[h][:, 0 : 2 * feat],
                preferred_element_type=jnp.float32,
            )
            for h in (0, 1)
        )
        sm_ref[...] = quarters_sum(wide, s_dev) / mass + center

    x_own = pieces[0][0:s_dev, :] - center
    sq_own = k * jnp.sum(x_own * x_own, axis=1, keepdims=True)

    for step in range(1, ITERS):
        v = tuple(m / t for m, t in zip(mass_b, total))
        clear()
        moved_parts = []
        for i in range(steps):
            kept, s = halves(i)
            e0, e1 = kept[0][s, :], kept[1][s, :]
            r = jnp.sum(e0 * v[0] + e1 * v[1], axis=1, keepdims=True)
            sums.extend(r[p * sub : (p + 1) * sub, :] for p in range(parts))
            u = la_col[i * blk : (i + 1) * blk, :] / r
            acc0[...] += column_part(e0, u)
            acc1[...] += column_part(e1, u)
            if step == ITERS - 1:
                moved_parts.append(target_sums(e0[:, 0:t_dev] * u, i))
                if i == 0:
                    u_own = u[0:s_dev, :]
        total = column_end()
    v = tuple(m / t for m, t in zip(mass_b, total))

    def put_f(f):
        wide = jnp.broadcast_to(f, (s_dev, feat))
        wide = jnp.concatenate([wide, jnp.zeros((feat - s_dev, feat), jnp.float32)], 0)
        f_ref[...] = wide.T[0:1, 0:s_dev]

    put_f(EPS * jnp.log(u_own) + (EPS * LN2) * (sq_own + shift))
    g_ref[...] = EPS * jnp.log(v[0][:, 0:t_dev])
    put_targets(moved_parts, total[0][:, 0:t_dev])
    put_sources((e11[0:s_dev, :] * v[0], e12[0:s_dev, :] * v[1]))

    low_r, high_r, low_c, high_c = least(sums), most(sums), least(ends), most(ends)
    bad = jnp.max(jnp.where((low_r < 1.0 / SAFE) | (high_r > WIDE), 1.0, 0.0)) + jnp.max(
        jnp.where((low_c < 1.0 / SAFE) | (high_c > SAFE), 1.0, 0.0)
    )
    finite = (jnp.max(high_r) < WIDE) & (jnp.max(high_c) < SAFE)

    @pl.when(jnp.logical_not((bad == 0.0) & finite))
    def _():
        quarters = ((e_own, e12), (e21, e22))

        def at_block(i):
            return pl.ds(pl.multiple_of(i * blk, blk), blk)

        for a in (0, 1):
            for h in (0, 1):

                def inner(i, carry):
                    s = at_block(i)
                    quarters[a][h][s, :] = nt_dot(xs[a][s, :], ys[h][...])
                    return carry

                lax.fori_loop(0, near, inner, 0)

        def potentials(step, g):
            for a in (0, 1):

                def row(i, carry):
                    s, line = at_block(i), at_block(i + a * near)
                    t = [quarters[a][h][s, :] + g[h] for h in (0, 1)]
                    top = jnp.max(jnp.maximum(t[0], t[1]), axis=1, keepdims=True)
                    mass = jnp.sum(jnp.exp2(t[0] - top) + jnp.exp2(t[1] - top), axis=1, keepdims=True)
                    u_col[line, :] = jnp.log2(la_col[line, :]) - top - jnp.log2(mass)
                    return carry

                lax.fori_loop(0, near, row, 0)

            new = []
            for h in (0, 1):
                top = jnp.full((1, half_t), -jnp.inf, jnp.float32)
                mass = jnp.zeros((1, half_t), jnp.float32)
                for a in (0, 1):

                    def column_top(i, top):
                        t = quarters[a][h][at_block(i), :] + u_col[at_block(i + a * near), :]
                        return jnp.maximum(top, jnp.max(t, axis=0, keepdims=True))

                    top = lax.fori_loop(0, near, column_top, top)
                for a in (0, 1):

                    def column_mass(i, mass):
                        t = quarters[a][h][at_block(i), :] + u_col[at_block(i + a * near), :]
                        return mass + jnp.sum(jnp.exp2(t - top), axis=0, keepdims=True)

                    mass = lax.fori_loop(0, near, column_mass, mass)
                new.append(jnp.log2(mass_b[h]) - top - jnp.log2(mass))
            return tuple(new)

        g = lax.fori_loop(0, ITERS, potentials, (-norms[0], -norms[1]))
        u_first = u_col[0:s_dev, :]
        put_f((EPS * LN2) * (u_first + sq_own))
        g_ref[...] = (EPS * LN2) * (g[0][:, 0:t_dev] + norms[0][:, 0:t_dev])
        put_sources([jnp.exp2(quarters[0][h][0:s_dev, :] + u_first + g[h]) for h in (0, 1)])

        def own_columns(i):
            at = (i % near) * blk
            inner = quarters[i // near][0][at : at + blk, 0:t_dev]
            return jnp.exp2(inner + u_col[i * blk : (i + 1) * blk, :] + g[0][:, 0:t_dev])

        mass = mass_b[0][:, 0:t_dev]
        put_targets([target_sums(own_columns(i), i) for i in range(steps)], mass)


def exchange(block, axis):
    n = lax.axis_size(axis)

    def swap(a, bits):
        return lax.ppermute(a, axis, [(i, i ^ bits) for i in range(n)])

    step = [swap(block, 4)]
    for bits in range(8, n, 8):
        jump = swap(block, bits)
        step += [jump, swap(jump, 4)]
    line = [block] + step
    side = [swap(a, 2) for a in line]
    return line + [swap(a, 1) for a in line], side + [swap(a, 1) for a in side]


def per_device_whole(source_feats, target_feats, log_a, log_b):
    n = lax.axis_size("src")
    s_dev, feat = source_feats.shape
    t_dev = target_feats.shape[0]
    masses = jnp.concatenate([log_b, log_a, jnp.zeros((8 * feat - t_dev - s_dev,), jnp.float32)])
    block = jnp.concatenate([source_feats, target_feats, masses.reshape(8, feat)], axis=0)
    block = lax.optimization_barrier(block)
    near_pieces, far_pieces = exchange(block, "src")
    sources, targets = n * s_dev, n * t_dev
    half_s, half_t = sources // 2, targets // 2
    blk = 256
    f32, b16 = jnp.float32, jnp.bfloat16
    vmem = pl.BlockSpec(memory_space=pltpu.VMEM)
    near = pl.pallas_call(
        functools.partial(near_kernel, s_dev, t_dev, blk),
        out_shape=[
            jax.ShapeDtypeStruct((half_s, half_t), f32),
            jax.ShapeDtypeStruct((half_s, 4 * feat), b16),
            jax.ShapeDtypeStruct((half_t, 4 * feat), b16),
            jax.ShapeDtypeStruct((half_s, 1), f32),
            jax.ShapeDtypeStruct((1, half_t), f32),
            jax.ShapeDtypeStruct((8, feat), f32),
        ],
        in_specs=[vmem] * len(near_pieces),
        out_specs=[vmem] * 6,
        scratch_shapes=[pltpu.VMEM((blk, half_t), f32), pltpu.VMEM((blk, half_t), f32)],
        compiler_params=pltpu.CompilerParams(vmem_limit_bytes=NEAR_VMEM),
        cost_estimate=pl.CostEstimate(
            flops=2 * half_s * half_t * 4 * feat,
            bytes_accessed=8 * 2**20,
            transcendentals=half_s * half_t,
        ),
        name="near",
    )(*near_pieces)
    f_pot, g_pot, src_moved, tgt_moved = pl.pallas_call(
        functools.partial(whole_group_kernel, n, s_dev, t_dev, blk),
        out_shape=[
            jax.ShapeDtypeStruct((1, s_dev), f32),
            jax.ShapeDtypeStruct((1, t_dev), f32),
            jax.ShapeDtypeStruct((s_dev, feat), f32),
            jax.ShapeDtypeStruct((t_dev, feat), f32),
        ],
        in_specs=[vmem] * (len(near_pieces) + len(far_pieces) + 6),
        out_specs=[vmem] * 4,
        scratch_shapes=[
            pltpu.VMEM((half_s, half_t), f32),
            pltpu.VMEM((half_s, half_t), f32),
            pltpu.VMEM((half_s, half_t), f32),
            pltpu.VMEM((half_s, half_t), f32),
            pltpu.VMEM((half_s, 4 * feat), b16),
            pltpu.VMEM((half_t, 4 * feat), b16),
            pltpu.VMEM((sources, 1), f32),
            pltpu.VMEM((sources, 1), f32),
            pltpu.VMEM((8, half_t), f32),
            pltpu.VMEM((8, half_t), f32),
            pltpu.VMEM((blk, targets), f32),
            pltpu.VMEM((blk, targets), f32),
        ],
        compiler_params=pltpu.CompilerParams(vmem_limit_bytes=WHOLE_VMEM),
        name="whole_group",
    )(*near_pieces, *far_pieces, *near)
    return f_pot.reshape(s_dev), g_pot.reshape(t_dev), src_moved, tgt_moved


def merged(part, axis, combine):
    gathered = jax.tree.map(lambda a: lax.all_gather(a, axis), part)

    def take(source):
        return jax.tree.map(lambda a: lax.dynamic_index_in_dim(a, source, 0, False), gathered)

    return lax.fori_loop(
        1, lax.axis_size(axis), lambda source, state: combine(state, take(source)), take(0)
    )


def pair_cost(rows, cols, rows_sq, cols_sq, width):
    inner = jnp.dot(rows, cols.T, precision=HI, preferred_element_type=jnp.float32)
    return (rows_sq[:, None] + cols_sq[None, :] - 2.0 * inner) / width


def row_update(cost, g_pot, log_mass):
    scores = (g_pot[None, :] - cost) / EPS
    top = jnp.max(scores, axis=1)
    total = jnp.sum(jnp.exp(scores - top[:, None]), axis=1)
    return EPS * log_mass - EPS * (top + jnp.log(total))


def combine_pairs(first, second):
    top = jnp.maximum(first[0], second[0])
    total = first[1] * jnp.exp(first[0] - top) + second[1] * jnp.exp(second[0] - top)
    return (top, total)


def per_device_rows(source_feats, target_feats, log_a, log_b):
    width = source_feats.shape[1]
    rows = target_feats.shape[0]
    tgt_all, log_b_all = (
        lax.all_gather(target_feats, "src", axis=0, tiled=True),
        lax.all_gather(log_b, "src", axis=0, tiled=True),
    )
    sq_src = jnp.sum(source_feats * source_feats, axis=1)
    sq_tgt = jnp.sum(tgt_all * tgt_all, axis=1)
    cost = pair_cost(source_feats, tgt_all, sq_src, sq_tgt, width)
    g_pot = jnp.zeros((tgt_all.shape[0],), jnp.float32)
    f_pot = jnp.zeros((source_feats.shape[0],), jnp.float32)
    for step in range(ITERS):
        f_pot = row_update(cost, g_pot, log_a)
        scores = (f_pot[:, None] - cost) / EPS
        local_top = jnp.max(scores, axis=0)
        local_total = jnp.sum(jnp.exp(scores - local_top[None, :]), axis=0)
        top, total = merged((local_top, local_total), "src", combine_pairs)
        g_pot = EPS * log_b_all - EPS * (top + jnp.log(total))
    plan = jnp.exp((f_pot[:, None] + g_pot[None, :] - cost) / EPS)
    carried = jnp.dot(plan, tgt_all, precision=HI, preferred_element_type=jnp.float32)
    src_moved = carried / jnp.sum(plan, axis=1)[:, None]
    own_start = lax.axis_index("src") * rows
    g_own = lax.dynamic_slice_in_dim(g_pot, own_start, rows)
    gathered = lax.psum_scatter(
        lax.dot_general(
            plan,
            source_feats,
            (((0,), (0,)), ((), ())),
            precision=HI,
            preferred_element_type=jnp.float32,
        ),
        "src",
        scatter_dimension=0,
        tiled=True,
    )
    tgt_moved = gathered / jnp.exp(log_b)[:, None]
    return (f_pot, g_own, src_moved, tgt_moved)


def per_device(source_feats, target_feats, log_a, log_b):
    n = lax.axis_size("src")
    s_dev, feat = source_feats.shape
    t_dev = target_feats.shape[0]
    fits = 4 * n * s_dev * n * t_dev <= REPLICATED_BYTES
    shaped = n >= 4 and n & (n - 1) == 0 and s_dev % 16 == 0 and s_dev <= feat == t_dev
    if fits and shaped and (n * s_dev) % 512 == 0 and n == 16:
        return per_device_whole(source_feats, target_feats, log_a, log_b)
    return per_device_rows(source_feats, target_feats, log_a, log_b)


def solution(mesh):
    both = P(("groups", "src"), None)
    line = P(("groups", "src"))
    return jax.shard_map(
        per_device,
        mesh=mesh,
        in_specs=(both, both, line, line),
        out_specs=(line, line, both, both),
        check_vma=False,
    )
```

```python
import functools

import jax
import jax.numpy as jnp
from jax import lax
from jax.experimental import pallas as pl
from jax.experimental.pallas import tpu as pltpu
from jax.sharding import PartitionSpec as P

ITERS = 3
EPS = 0.05
LN2 = 0.6931471805599453
LOG2E = 1.4426950408889634
SAFE = 2.0**30
WIDE = 2.0**60
PARTS = 4
CHUNK = 256
NEAR_VMEM = 16 * 2**20
WHOLE_VMEM = 36 * 2**20
REPLICATED_BYTES = 24 * 2**20
HI = lax.Precision.HIGHEST


def split3(a):
    first = a.astype(jnp.bfloat16)
    rest = a - first.astype(jnp.float32)
    second = rest.astype(jnp.bfloat16)
    third = (rest - second.astype(jnp.float32)).astype(jnp.bfloat16)
    return first, second, third


def split2(a):
    first = a.astype(jnp.bfloat16)
    return first, (a - first.astype(jnp.float32)).astype(jnp.bfloat16)


def nt_dot(a, b, precision=None):
    return lax.dot_general(
        a, b, (((1,), (1,)), ((), ())), precision=precision, preferred_element_type=jnp.float32
    )


def least(values):
    return functools.reduce(jnp.minimum, values)


def most(values):
    return functools.reduce(jnp.maximum, values)


def blocks_of(pieces, rows):
    return [(ref, at) for ref in pieces for at in range(0, ref.shape[0], rows)]


def target_sum(blocks, s_dev, t_dev):
    total = sum(
        jnp.sum(ref[at + s_dev : at + s_dev + t_dev, :].reshape(t_dev // 8, 8, -1), axis=0)
        for ref, at in blocks
    )
    return jnp.sum(total, axis=0, keepdims=True)


def split_features(blocks, s_dev, t_dev, center, k, xs, ys):
    feat = center.shape[1]
    norms = []
    ones = jnp.ones((8, 3 * feat), jnp.bfloat16)
    for d, (ref, at) in enumerate(blocks):
        x1, x2 = split2((ref[at : at + s_dev, :] - center) * (2.0 * k))
        xs[d * s_dev : (d + 1) * s_dev, :] = jnp.concatenate([x1, x1, x2, x2], 1)
        y = ref[at + s_dev : at + s_dev + t_dev, :] - center
        y1, y2 = split2(y)
        ys[d * t_dev : (d + 1) * t_dev, :] = jnp.concatenate([y1, y2, y1, y2], 1)
        norms.append(nt_dot(ones, jnp.concatenate(split3(y * y), 1))[0:1, :])
    return jnp.concatenate(norms, 1) * k


def near_kernel(s_dev, t_dev, blk, *refs):
    pieces = refs[:-6]
    e_ref, xs, ys, r_ref, norm_ref, mid_ref = refs[-6:]
    feat = pieces[0].shape[1]
    k = LOG2E / (feat * EPS)
    blocks = blocks_of(pieces, s_dev + t_dev + 8)
    sources, targets = len(blocks) * s_dev, len(blocks) * t_dev
    center = target_sum(blocks, s_dev, t_dev) * (1.0 / targets)
    norm = split_features(blocks, s_dev, t_dev, center, k, xs, ys)
    norm_ref[...] = norm
    shift = jnp.mean(norm, axis=1, keepdims=True)
    mid_ref[0:1, :] = center
    mid_ref[1:2, :] = jnp.broadcast_to(shift, (1, feat))
    mid_ref[2:8, :] = jnp.zeros((6, feat), jnp.float32)
    g1 = shift - norm
    for i in range(sources // blk):
        s = slice(i * blk, (i + 1) * blk)
        row_sum = 0.0
        for c in range(0, targets, CHUNK):
            cols = slice(c, c + CHUNK)
            e = jnp.exp2(nt_dot(xs[s, :], ys[cols, :]) + g1[:, cols])
            e_ref[s, cols] = e
            row_sum += sum(e[:, c : c + feat] for c in range(0, CHUNK, feat))
        r_ref[s, :] = jnp.sum(row_sum, axis=1, keepdims=True)


def whole_group_kernel(n, s_dev, t_dev, blk, *refs):
    pieces = refs[:-20]
    e11, xs1, ys1, r1_ref, norm_ref, mid_ref = refs[-20:-14]
    f_ref, g_ref, sm_ref, tm_ref = refs[-14:-10]
    e12, e21, e22, e_own, xs2, ys2, la_col, u_col, acc0, acc1 = refs[-10:]
    feat = pieces[0].shape[1]
    rows = s_dev + t_dev + 8
    k = LOG2E / (feat * EPS)
    sources, targets = n * s_dev, n * t_dev
    half_s, half_t = sources // 2, targets // 2
    xs, ys, accs = (xs1, xs2), (ys1, ys2), (acc0, acc1)

    blocks = blocks_of(pieces, rows)
    center = mid_ref[0:1, :]
    shift = mid_ref[1:2, 0:1]
    norms = (norm_ref[...], split_features(blocks[n // 2 :], s_dev, t_dev, center, k, xs2, ys2))
    lbs = [ref[at + s_dev + t_dev : at + s_dev + t_dev + 1, :] for ref, at in blocks]
    las = [ref[at + s_dev + t_dev + 1 : at + s_dev + t_dev + 2, :] for ref, at in blocks]
    g1 = tuple(shift - norm for norm in norms)
    mass_b = tuple(jnp.exp(jnp.concatenate(part, 1)) for part in (lbs[: n // 2], lbs[n // 2 :]))
    la_t = jnp.exp(jnp.concatenate(las, 0)).T
    for d in range(n):
        la_col[d * s_dev : (d + 1) * s_dev, :] = la_t[:s_dev, d : d + 1]

    steps = sources // blk
    near = steps // 2
    parts = PARTS
    sub = blk // parts

    def halves(i, first=e11):
        at = (i % near) * blk
        return ((first, e12) if i < near else (e21, e22)), slice(at, at + blk)

    def column_part(e, u):
        return jnp.sum((e * u).reshape(e.shape[0] // 8, 8, half_t), axis=0)

    row_sums = [0.0] * steps

    def product(i, part):
        kept, where = halves(i)
        factor = xs[i // near][where, :]
        chunks = [
            (h, slice(c, c + CHUNK))
            for h in ((1,) if i < near else (0, 1))
            for c in range(0, half_t, CHUNK)
        ]
        for h, cols in chunks[part * len(chunks) // parts : (part + 1) * len(chunks) // parts]:
            e = jnp.exp2(nt_dot(factor, ys[h][cols, :]) + g1[h][:, cols])
            kept[h][where, cols] = e
            row_sums[i] += sum(e[:, c : c + feat] for c in range(0, CHUNK, feat))

    sums, ends = [], []

    def absorb(i, part):
        kept, where = halves(i)
        local = slice(part * sub, (part + 1) * sub)
        s = slice(where.start + local.start, where.start + local.stop)
        r = jnp.sum(row_sums[i][local, :], axis=1, keepdims=True)
        if i < near:
            r = r + r1_ref[s, :]
        sums.append(r)
        u = la_col[i * blk + local.start : i * blk + local.stop, :] / r
        acc0[...] += column_part(kept[0][s, :], u)
        acc1[...] += column_part(kept[1][s, :], u)

    def column_end():
        total = tuple(jnp.sum(acc[...], axis=0, keepdims=True) for acc in accs)
        ends.extend(total)
        return total

    def clear():
        for acc in accs:
            acc[...] = jnp.zeros_like(acc)

    clear()
    for part in range(parts):
        product(0, part)
    for i in range(steps):
        for part in range(parts):
            if i + 1 < steps:
                product(i + 1, part)
            absorb(i, part)
    total = column_end()

    def quarters_sum(wide, count):
        low = wide[:count, feat:] + (wide[count:, :feat] + wide[count:, feat:])
        return wide[:count, :feat] + low

    def target_sums(plan, i):
        at = (i % near) * blk
        return lax.dot_general(
            jnp.concatenate(split2(plan), 1),
            xs[i // near][at : at + blk, feat : 3 * feat],
            (((0,), (0,)), ((), ())),
            preferred_element_type=jnp.float32,
        )

    def put_targets(sums_of, mass):
        moved = quarters_sum(sum(sums_of), t_dev)
        mass = jnp.broadcast_to(mass * (2.0 * k), (feat, t_dev)).T
        tm_ref[...] = moved / mass + center

    def put_sources(plan):
        mass = jnp.sum(plan[0] + plan[1], axis=1, keepdims=True)
        wide = sum(
            jnp.dot(
                jnp.concatenate(split2(plan[h]), 0),
                ys[h][:, 0 : 2 * feat],
                preferred_element_type=jnp.float32,
            )
            for h in (0, 1)
        )
        sm_ref[...] = quarters_sum(wide, s_dev) / mass + center

    x_own = pieces[0][0:s_dev, :] - center
    sq_own = k * jnp.sum(x_own * x_own, axis=1, keepdims=True)

    for step in range(1, ITERS):
        v = tuple(m / t for m, t in zip(mass_b, total))
        clear()
        moved_parts = []
        for i in range(steps):
            kept, s = halves(i)
            e0, e1 = kept[0][s, :], kept[1][s, :]
            r = jnp.sum(e0 * v[0] + e1 * v[1], axis=1, keepdims=True)
            sums.extend(r[p * sub : (p + 1) * sub, :] for p in range(parts))
            u = la_col[i * blk : (i + 1) * blk, :] / r
            acc0[...] += column_part(e0, u)
            acc1[...] += column_part(e1, u)
            if step == ITERS - 1:
                moved_parts.append(target_sums(e0[:, 0:t_dev] * u, i))
                if i == 0:
                    u_own = u[0:s_dev, :]
        total = column_end()
    v = tuple(m / t for m, t in zip(mass_b, total))

    def put_f(f):
        wide = jnp.broadcast_to(f, (s_dev, feat))
        wide = jnp.concatenate([wide, jnp.zeros((feat - s_dev, feat), jnp.float32)], 0)
        f_ref[...] = wide.T[0:1, 0:s_dev]

    put_f(EPS * jnp.log(u_own) + (EPS * LN2) * (sq_own + shift))
    g_ref[...] = EPS * jnp.log(v[0][:, 0:t_dev])
    put_targets(moved_parts, total[0][:, 0:t_dev])
    put_sources((e11[0:s_dev, :] * v[0], e12[0:s_dev, :] * v[1]))

    low_r, high_r, low_c, high_c = least(sums), most(sums), least(ends), most(ends)
    bad = jnp.max(jnp.where((low_r < 1.0 / SAFE) | (high_r > WIDE), 1.0, 0.0)) + jnp.max(
        jnp.where((low_c < 1.0 / SAFE) | (high_c > SAFE), 1.0, 0.0)
    )
    finite = (jnp.max(high_r) < WIDE) & (jnp.max(high_c) < SAFE)

    @pl.when(jnp.logical_not((bad == 0.0) & finite))
    def _():
        quarters = ((e_own, e12), (e21, e22))

        def at_block(i):
            return pl.ds(pl.multiple_of(i * blk, blk), blk)

        for a in (0, 1):
            for h in (0, 1):

                def inner(i, carry):
                    s = at_block(i)
                    quarters[a][h][s, :] = nt_dot(xs[a][s, :], ys[h][...])
                    return carry

                lax.fori_loop(0, near, inner, 0)

        def potentials(step, g):
            for a in (0, 1):

                def row(i, carry):
                    s, line = at_block(i), at_block(i + a * near)
                    t = [quarters[a][h][s, :] + g[h] for h in (0, 1)]
                    top = jnp.max(jnp.maximum(t[0], t[1]), axis=1, keepdims=True)
                    mass = jnp.sum(jnp.exp2(t[0] - top) + jnp.exp2(t[1] - top), axis=1, keepdims=True)
                    u_col[line, :] = jnp.log2(la_col[line, :]) - top - jnp.log2(mass)
                    return carry

                lax.fori_loop(0, near, row, 0)

            new = []
            for h in (0, 1):
                top = jnp.full((1, half_t), -jnp.inf, jnp.float32)
                mass = jnp.zeros((1, half_t), jnp.float32)
                for a in (0, 1):

                    def column_top(i, top):
                        t = quarters[a][h][at_block(i), :] + u_col[at_block(i + a * near), :]
                        return jnp.maximum(top, jnp.max(t, axis=0, keepdims=True))

                    top = lax.fori_loop(0, near, column_top, top)
                for a in (0, 1):

                    def column_mass(i, mass):
                        t = quarters[a][h][at_block(i), :] + u_col[at_block(i + a * near), :]
                        return mass + jnp.sum(jnp.exp2(t - top), axis=0, keepdims=True)

                    mass = lax.fori_loop(0, near, column_mass, mass)
                new.append(jnp.log2(mass_b[h]) - top - jnp.log2(mass))
            return tuple(new)

        g = lax.fori_loop(0, ITERS, potentials, (-norms[0], -norms[1]))
        u_first = u_col[0:s_dev, :]
        put_f((EPS * LN2) * (u_first + sq_own))
        g_ref[...] = (EPS * LN2) * (g[0][:, 0:t_dev] + norms[0][:, 0:t_dev])
        put_sources([jnp.exp2(quarters[0][h][0:s_dev, :] + u_first + g[h]) for h in (0, 1)])

        def own_columns(i):
            at = (i % near) * blk
            inner = quarters[i // near][0][at : at + blk, 0:t_dev]
            return jnp.exp2(inner + u_col[i * blk : (i + 1) * blk, :] + g[0][:, 0:t_dev])

        mass = mass_b[0][:, 0:t_dev]
        put_targets([target_sums(own_columns(i), i) for i in range(steps)], mass)


def exchange(block, axis):
    n = lax.axis_size(axis)

    def swap(a, bits):
        return lax.ppermute(a, axis, [(i, i ^ bits) for i in range(n)])

    near, jump = swap(block, 4), swap(block, 8)
    across = swap(block, 2)
    last, over = swap(jump, 4), swap(jump, 2)
    line = [block, near, jump, last]
    side = [across, swap(near, 2), over, swap(over, 4)]
    return line + [swap(a, 1) for a in line], side + [swap(a, 1) for a in side]


def per_device_whole(source_feats, target_feats, log_a, log_b):
    n = lax.axis_size("src")
    s_dev, feat = source_feats.shape
    t_dev = target_feats.shape[0]
    masses = jnp.concatenate([log_b, log_a, jnp.zeros((8 * feat - t_dev - s_dev,), jnp.float32)])
    block = jnp.concatenate([source_feats, target_feats, masses.reshape(8, feat)], axis=0)
    block = lax.optimization_barrier(block)
    near_pieces, far_pieces = exchange(block, "src")
    sources, targets = n * s_dev, n * t_dev
    half_s, half_t = sources // 2, targets // 2
    blk = 256
    f32, b16 = jnp.float32, jnp.bfloat16
    vmem = pl.BlockSpec(memory_space=pltpu.VMEM)
    near = pl.pallas_call(
        functools.partial(near_kernel, s_dev, t_dev, blk),
        out_shape=[
            jax.ShapeDtypeStruct((half_s, half_t), f32),
            jax.ShapeDtypeStruct((half_s, 4 * feat), b16),
            jax.ShapeDtypeStruct((half_t, 4 * feat), b16),
            jax.ShapeDtypeStruct((half_s, 1), f32),
            jax.ShapeDtypeStruct((1, half_t), f32),
            jax.ShapeDtypeStruct((8, feat), f32),
        ],
        in_specs=[vmem] * len(near_pieces),
        out_specs=[vmem] * 6,
        compiler_params=pltpu.CompilerParams(vmem_limit_bytes=NEAR_VMEM),
        cost_estimate=pl.CostEstimate(
            flops=2 * half_s * half_t * 4 * feat,
            bytes_accessed=8 * 2**20,
            transcendentals=half_s * half_t,
        ),
        name="near",
    )(*near_pieces)
    f_pot, g_pot, src_moved, tgt_moved = pl.pallas_call(
        functools.partial(whole_group_kernel, n, s_dev, t_dev, blk),
        out_shape=[
            jax.ShapeDtypeStruct((1, s_dev), f32),
            jax.ShapeDtypeStruct((1, t_dev), f32),
            jax.ShapeDtypeStruct((s_dev, feat), f32),
            jax.ShapeDtypeStruct((t_dev, feat), f32),
        ],
        in_specs=[vmem] * (len(near_pieces) + len(far_pieces) + 6),
        out_specs=[vmem] * 4,
        scratch_shapes=[
            pltpu.VMEM((half_s, half_t), f32),
            pltpu.VMEM((half_s, half_t), f32),
            pltpu.VMEM((half_s, half_t), f32),
            pltpu.VMEM((half_s, half_t), f32),
            pltpu.VMEM((half_s, 4 * feat), b16),
            pltpu.VMEM((half_t, 4 * feat), b16),
            pltpu.VMEM((sources, 1), f32),
            pltpu.VMEM((sources, 1), f32),
            pltpu.VMEM((8, half_t), f32),
            pltpu.VMEM((8, half_t), f32),
        ],
        compiler_params=pltpu.CompilerParams(vmem_limit_bytes=WHOLE_VMEM),
        name="whole_group",
    )(*near_pieces, *far_pieces, *near)
    return f_pot.reshape(s_dev), g_pot.reshape(t_dev), src_moved, tgt_moved


def merged(part, axis, combine):
    gathered = jax.tree.map(lambda a: lax.all_gather(a, axis), part)

    def take(source):
        return jax.tree.map(lambda a: lax.dynamic_index_in_dim(a, source, 0, False), gathered)

    return lax.fori_loop(
        1, lax.axis_size(axis), lambda source, state: combine(state, take(source)), take(0)
    )


def pair_cost(rows, cols, rows_sq, cols_sq, width):
    inner = jnp.dot(rows, cols.T, precision=HI, preferred_element_type=jnp.float32)
    return (rows_sq[:, None] + cols_sq[None, :] - 2.0 * inner) / width


def row_update(cost, g_pot, log_mass):
    scores = (g_pot[None, :] - cost) / EPS
    top = jnp.max(scores, axis=1)
    total = jnp.sum(jnp.exp(scores - top[:, None]), axis=1)
    return EPS * log_mass - EPS * (top + jnp.log(total))


def combine_pairs(first, second):
    top = jnp.maximum(first[0], second[0])
    total = first[1] * jnp.exp(first[0] - top) + second[1] * jnp.exp(second[0] - top)
    return (top, total)


def per_device_rows(source_feats, target_feats, log_a, log_b):
    width = source_feats.shape[1]
    rows = target_feats.shape[0]
    tgt_all, log_b_all = (
        lax.all_gather(target_feats, "src", axis=0, tiled=True),
        lax.all_gather(log_b, "src", axis=0, tiled=True),
    )
    sq_src = jnp.sum(source_feats * source_feats, axis=1)
    sq_tgt = jnp.sum(tgt_all * tgt_all, axis=1)
    cost = pair_cost(source_feats, tgt_all, sq_src, sq_tgt, width)
    g_pot = jnp.zeros((tgt_all.shape[0],), jnp.float32)
    f_pot = jnp.zeros((source_feats.shape[0],), jnp.float32)
    for step in range(ITERS):
        f_pot = row_update(cost, g_pot, log_a)
        scores = (f_pot[:, None] - cost) / EPS
        local_top = jnp.max(scores, axis=0)
        local_total = jnp.sum(jnp.exp(scores - local_top[None, :]), axis=0)
        top, total = merged((local_top, local_total), "src", combine_pairs)
        g_pot = EPS * log_b_all - EPS * (top + jnp.log(total))
    plan = jnp.exp((f_pot[:, None] + g_pot[None, :] - cost) / EPS)
    carried = jnp.dot(plan, tgt_all, precision=HI, preferred_element_type=jnp.float32)
    src_moved = carried / jnp.sum(plan, axis=1)[:, None]
    own_start = lax.axis_index("src") * rows
    g_own = lax.dynamic_slice_in_dim(g_pot, own_start, rows)
    gathered = lax.psum_scatter(
        lax.dot_general(
            plan,
            source_feats,
            (((0,), (0,)), ((), ())),
            precision=HI,
            preferred_element_type=jnp.float32,
        ),
        "src",
        scatter_dimension=0,
        tiled=True,
    )
    tgt_moved = gathered / jnp.exp(log_b)[:, None]
    return (f_pot, g_own, src_moved, tgt_moved)


def per_device(source_feats, target_feats, log_a, log_b):
    n = lax.axis_size("src")
    s_dev, feat = source_feats.shape
    t_dev = target_feats.shape[0]
    fits = 4 * n * s_dev * n * t_dev <= REPLICATED_BYTES
    shaped = n >= 4 and n & (n - 1) == 0 and s_dev % 16 == 0 and s_dev <= feat == t_dev
    if fits and shaped and (n * s_dev) % 512 == 0 and n == 16:
        return per_device_whole(source_feats, target_feats, log_a, log_b)
    return per_device_rows(source_feats, target_feats, log_a, log_b)


def solution(mesh):
    both = P(("groups", "src"), None)
    line = P(("groups", "src"))
    return jax.shard_map(
        per_device,
        mesh=mesh,
        in_specs=(both, both, line, line),
        out_specs=(line, line, both, both),
        check_vma=False,
    )
```

```python
import functools

import jax
import jax.numpy as jnp
from jax import lax
from jax.experimental import pallas as pl
from jax.experimental.pallas import tpu as pltpu
from jax.sharding import PartitionSpec as P

ITERS = 3
EPS = 0.05
LN2 = 0.6931471805599453
LOG2E = 1.4426950408889634
SAFE = 2.0**30
WIDE = 2.0**60
PARTS = 4
CHUNK = 256
NEAR_VMEM = 16 * 2**20
WHOLE_VMEM = 36 * 2**20
REPLICATED_BYTES = 24 * 2**20
HI = lax.Precision.HIGHEST


def split3(a):
    first = a.astype(jnp.bfloat16)
    rest = a - first.astype(jnp.float32)
    second = rest.astype(jnp.bfloat16)
    third = (rest - second.astype(jnp.float32)).astype(jnp.bfloat16)
    return first, second, third


def split2(a):
    first = a.astype(jnp.bfloat16)
    return first, (a - first.astype(jnp.float32)).astype(jnp.bfloat16)


def nt_dot(a, b, precision=None):
    return lax.dot_general(
        a, b, (((1,), (1,)), ((), ())), precision=precision, preferred_element_type=jnp.float32
    )


def least(values):
    return functools.reduce(jnp.minimum, values)


def most(values):
    return functools.reduce(jnp.maximum, values)


def blocks_of(pieces, rows):
    return [(ref, at) for ref in pieces for at in range(0, ref.shape[0], rows)]


def target_sum(blocks, s_dev, t_dev):
    total = sum(
        jnp.sum(ref[at + s_dev : at + s_dev + t_dev, :].reshape(t_dev // 8, 8, -1), axis=0)
        for ref, at in blocks
    )
    return jnp.sum(total, axis=0, keepdims=True)


def split_features(blocks, s_dev, t_dev, center, k, xs, ys):
    feat = center.shape[1]
    norms = []
    ones = jnp.ones((8, 3 * feat), jnp.bfloat16)
    for d, (ref, at) in enumerate(blocks):
        x1, x2 = split2((ref[at : at + s_dev, :] - center) * (2.0 * k))
        xs[d * s_dev : (d + 1) * s_dev, :] = jnp.concatenate([x1, x1, x2, x2], 1)
        y = ref[at + s_dev : at + s_dev + t_dev, :] - center
        y1, y2 = split2(y)
        ys[d * t_dev : (d + 1) * t_dev, :] = jnp.concatenate([y1, y2, y1, y2], 1)
        norms.append(nt_dot(ones, jnp.concatenate(split3(y * y), 1))[0:1, :])
    return jnp.concatenate(norms, 1) * k


def near_kernel(s_dev, t_dev, blk, *refs):
    pieces = refs[:-6]
    e_ref, xs, ys, r_ref, norm_ref, mid_ref = refs[-6:]
    feat = pieces[0].shape[1]
    k = LOG2E / (feat * EPS)
    blocks = blocks_of(pieces, s_dev + t_dev + 8)
    sources, targets = len(blocks) * s_dev, len(blocks) * t_dev
    center = target_sum(blocks, s_dev, t_dev) * (1.0 / targets)
    norm = split_features(blocks, s_dev, t_dev, center, k, xs, ys)
    norm_ref[...] = norm
    shift = jnp.mean(norm, axis=1, keepdims=True)
    mid_ref[0:1, :] = center
    mid_ref[1:2, :] = jnp.broadcast_to(shift, (1, feat))
    mid_ref[2:8, :] = jnp.zeros((6, feat), jnp.float32)
    g1 = shift - norm
    for i in range(sources // blk):
        s = slice(i * blk, (i + 1) * blk)
        row_sum = 0.0
        for c in range(0, targets, CHUNK):
            cols = slice(c, c + CHUNK)
            e = jnp.exp2(nt_dot(xs[s, :], ys[cols, :]) + g1[:, cols])
            e_ref[s, cols] = e
            row_sum += sum(e[:, c : c + feat] for c in range(0, CHUNK, feat))
        r_ref[s, :] = jnp.sum(row_sum, axis=1, keepdims=True)


def whole_group_kernel(n, s_dev, t_dev, blk, *refs):
    pieces = refs[:-20]
    e11, xs1, ys1, r1_ref, norm_ref, mid_ref = refs[-20:-14]
    f_ref, g_ref, sm_ref, tm_ref = refs[-14:-10]
    e12, e21, e22, e_own, xs2, ys2, la_col, u_col, acc0, acc1 = refs[-10:]
    feat = pieces[0].shape[1]
    rows = s_dev + t_dev + 8
    k = LOG2E / (feat * EPS)
    sources, targets = n * s_dev, n * t_dev
    half_s, half_t = sources // 2, targets // 2
    xs, ys, accs = (xs1, xs2), (ys1, ys2), (acc0, acc1)

    blocks = blocks_of(pieces, rows)
    center = mid_ref[0:1, :]
    shift = mid_ref[1:2, 0:1]
    norms = (norm_ref[...], split_features(blocks[n // 2 :], s_dev, t_dev, center, k, xs2, ys2))
    lbs = [ref[at + s_dev + t_dev : at + s_dev + t_dev + 1, :] for ref, at in blocks]
    las = [ref[at + s_dev + t_dev + 1 : at + s_dev + t_dev + 2, :] for ref, at in blocks]
    g1 = tuple(shift - norm for norm in norms)
    mass_b = tuple(jnp.exp(jnp.concatenate(part, 1)) for part in (lbs[: n // 2], lbs[n // 2 :]))
    la_t = jnp.exp(jnp.concatenate(las, 0)).T
    for d in range(n):
        la_col[d * s_dev : (d + 1) * s_dev, :] = la_t[:s_dev, d : d + 1]

    steps = sources // blk
    near = steps // 2
    parts = PARTS
    sub = blk // parts

    def halves(i, first=e11):
        at = (i % near) * blk
        return ((first, e12) if i < near else (e21, e22)), slice(at, at + blk)

    def column_part(e, u):
        return jnp.sum((e * u).reshape(e.shape[0] // 8, 8, half_t), axis=0)

    row_sums = [0.0] * steps

    def product(i, part):
        kept, where = halves(i)
        factor = xs[i // near][where, :]
        chunks = [
            (h, slice(c, c + CHUNK))
            for h in ((1,) if i < near else (0, 1))
            for c in range(0, half_t, CHUNK)
        ]
        for h, cols in chunks[part * len(chunks) // parts : (part + 1) * len(chunks) // parts]:
            e = jnp.exp2(nt_dot(factor, ys[h][cols, :]) + g1[h][:, cols])
            kept[h][where, cols] = e
            row_sums[i] += sum(e[:, c : c + feat] for c in range(0, CHUNK, feat))

    sums, ends = [], []

    def absorb(i, part):
        kept, where = halves(i)
        local = slice(part * sub, (part + 1) * sub)
        s = slice(where.start + local.start, where.start + local.stop)
        r = jnp.sum(row_sums[i][local, :], axis=1, keepdims=True)
        if i < near:
            r = r + r1_ref[s, :]
        sums.append(r)
        u = la_col[i * blk + local.start : i * blk + local.stop, :] / r
        acc0[...] += column_part(kept[0][s, :], u)
        acc1[...] += column_part(kept[1][s, :], u)

    def column_end():
        total = tuple(jnp.sum(acc[...], axis=0, keepdims=True) for acc in accs)
        ends.extend(total)
        return total

    def clear():
        for acc in accs:
            acc[...] = jnp.zeros_like(acc)

    clear()
    for part in range(parts):
        product(0, part)
    for i in range(steps):
        for part in range(parts):
            if i + 1 < steps:
                product(i + 1, part)
            absorb(i, part)
    total = column_end()

    def quarters_sum(wide, count):
        low = wide[:count, feat:] + (wide[count:, :feat] + wide[count:, feat:])
        return wide[:count, :feat] + low

    def target_sums(plan, i):
        at = (i % near) * blk
        return lax.dot_general(
            jnp.concatenate(split2(plan), 1),
            xs[i // near][at : at + blk, feat : 3 * feat],
            (((0,), (0,)), ((), ())),
            preferred_element_type=jnp.float32,
        )

    def put_targets(sums_of, mass):
        moved = quarters_sum(sum(sums_of), t_dev)
        mass = jnp.broadcast_to(mass * (2.0 * k), (feat, t_dev)).T
        tm_ref[...] = moved / mass + center

    def put_sources(plan):
        mass = jnp.sum(plan[0] + plan[1], axis=1, keepdims=True)
        wide = sum(
            jnp.dot(
                jnp.concatenate(split2(plan[h]), 0),
                ys[h][:, 0 : 2 * feat],
                preferred_element_type=jnp.float32,
            )
            for h in (0, 1)
        )
        sm_ref[...] = quarters_sum(wide, s_dev) / mass + center

    x_own = pieces[0][0:s_dev, :] - center
    sq_own = k * jnp.sum(x_own * x_own, axis=1, keepdims=True)

    for step in range(1, ITERS):
        v = tuple(m / t for m, t in zip(mass_b, total))
        clear()
        moved_parts = []
        for i in range(steps):
            kept, s = halves(i)
            e0, e1 = kept[0][s, :], kept[1][s, :]
            r = jnp.sum(e0 * v[0] + e1 * v[1], axis=1, keepdims=True)
            sums.extend(r[p * sub : (p + 1) * sub, :] for p in range(parts))
            u = la_col[i * blk : (i + 1) * blk, :] / r
            acc0[...] += column_part(e0, u)
            acc1[...] += column_part(e1, u)
            if step == ITERS - 1:
                moved_parts.append(target_sums(e0[:, 0:t_dev] * u, i))
                if i == 0:
                    u_own = u[0:s_dev, :]
        total = column_end()
    v = tuple(m / t for m, t in zip(mass_b, total))

    def put_f(f):
        wide = jnp.broadcast_to(f, (s_dev, feat))
        wide = jnp.concatenate([wide, jnp.zeros((feat - s_dev, feat), jnp.float32)], 0)
        f_ref[...] = wide.T[0:1, 0:s_dev]

    put_f(EPS * jnp.log(u_own) + (EPS * LN2) * (sq_own + shift))
    g_ref[...] = EPS * jnp.log(v[0][:, 0:t_dev])
    put_targets(moved_parts, total[0][:, 0:t_dev])
    put_sources((e11[0:s_dev, :] * v[0], e12[0:s_dev, :] * v[1]))

    low_r, high_r, low_c, high_c = least(sums), most(sums), least(ends), most(ends)
    bad = jnp.max(jnp.where((low_r < 1.0 / SAFE) | (high_r > WIDE), 1.0, 0.0)) + jnp.max(
        jnp.where((low_c < 1.0 / SAFE) | (high_c > SAFE), 1.0, 0.0)
    )
    finite = (jnp.max(high_r) < WIDE) & (jnp.max(high_c) < SAFE)

    @pl.when(jnp.logical_not((bad == 0.0) & finite))
    def _():
        quarters = ((e_own, e12), (e21, e22))

        def at_block(i):
            return pl.ds(pl.multiple_of(i * blk, blk), blk)

        for a in (0, 1):
            for h in (0, 1):

                def inner(i, carry):
                    s = at_block(i)
                    quarters[a][h][s, :] = nt_dot(xs[a][s, :], ys[h][...])
                    return carry

                lax.fori_loop(0, near, inner, 0)

        def potentials(step, g):
            for a in (0, 1):

                def row(i, carry):
                    s, line = at_block(i), at_block(i + a * near)
                    t = [quarters[a][h][s, :] + g[h] for h in (0, 1)]
                    top = jnp.max(jnp.maximum(t[0], t[1]), axis=1, keepdims=True)
                    mass = jnp.sum(jnp.exp2(t[0] - top) + jnp.exp2(t[1] - top), axis=1, keepdims=True)
                    u_col[line, :] = jnp.log2(la_col[line, :]) - top - jnp.log2(mass)
                    return carry

                lax.fori_loop(0, near, row, 0)

            new = []
            for h in (0, 1):
                top = jnp.full((1, half_t), -jnp.inf, jnp.float32)
                mass = jnp.zeros((1, half_t), jnp.float32)
                for a in (0, 1):

                    def column_top(i, top):
                        t = quarters[a][h][at_block(i), :] + u_col[at_block(i + a * near), :]
                        return jnp.maximum(top, jnp.max(t, axis=0, keepdims=True))

                    top = lax.fori_loop(0, near, column_top, top)
                for a in (0, 1):

                    def column_mass(i, mass):
                        t = quarters[a][h][at_block(i), :] + u_col[at_block(i + a * near), :]
                        return mass + jnp.sum(jnp.exp2(t - top), axis=0, keepdims=True)

                    mass = lax.fori_loop(0, near, column_mass, mass)
                new.append(jnp.log2(mass_b[h]) - top - jnp.log2(mass))
            return tuple(new)

        g = lax.fori_loop(0, ITERS, potentials, (-norms[0], -norms[1]))
        u_first = u_col[0:s_dev, :]
        put_f((EPS * LN2) * (u_first + sq_own))
        g_ref[...] = (EPS * LN2) * (g[0][:, 0:t_dev] + norms[0][:, 0:t_dev])
        put_sources([jnp.exp2(quarters[0][h][0:s_dev, :] + u_first + g[h]) for h in (0, 1)])

        def own_columns(i):
            at = (i % near) * blk
            inner = quarters[i // near][0][at : at + blk, 0:t_dev]
            return jnp.exp2(inner + u_col[i * blk : (i + 1) * blk, :] + g[0][:, 0:t_dev])

        mass = mass_b[0][:, 0:t_dev]
        put_targets([target_sums(own_columns(i), i) for i in range(steps)], mass)


def exchange(block, axis):
    n = lax.axis_size(axis)

    def swap(a, bits):
        return lax.ppermute(a, axis, [(i, i ^ bits) for i in range(n)])

    near, jump = swap(block, 4), swap(block, 8)
    across = swap(block, 2)
    last, over = swap(jump, 4), swap(jump, 2)
    line = [block, near, jump, last]
    side = [across, swap(near, 2), over, swap(over, 4)]
    return line + [swap(a, 1) for a in line], side + [swap(a, 1) for a in side]


def pack_kernel(x_ref, y_ref, la_ref, lb_ref, out_ref, la_row, lb_row, sems):
    s_dev, t_dev = x_ref.shape[0], y_ref.shape[0]
    rows = s_dev + t_dev
    copies = [
        pltpu.make_async_copy(src, dst, sems.at[i])
        for i, (src, dst) in enumerate(
            (
                (x_ref, out_ref.at[0:s_dev, :]),
                (y_ref, out_ref.at[s_dev:rows, :]),
                (la_ref, la_row),
                (lb_ref, lb_row),
            )
        )
    ]
    for copy in copies:
        copy.start()
    out_ref[rows:, :] = jnp.zeros((8, x_ref.shape[1]), jnp.float32)
    copies[2].wait()
    out_ref[rows + 1 : rows + 2, 0:s_dev] = la_row[...].reshape(1, s_dev)
    copies[3].wait()
    out_ref[rows : rows + 1, :] = lb_row[...].reshape(1, t_dev)
    copies[0].wait()
    copies[1].wait()


def per_device_whole(source_feats, target_feats, log_a, log_b):
    n = lax.axis_size("src")
    s_dev, feat = source_feats.shape
    t_dev = target_feats.shape[0]
    fixed = [pltpu.with_memory_space_constraint(a, pltpu.HBM) for a in (source_feats, target_feats, log_a, log_b)]
    block = pl.pallas_call(
        pack_kernel,
        out_shape=pltpu.VMEM((s_dev + t_dev + 8, feat), jnp.float32),
        in_specs=[pl.BlockSpec(memory_space=pltpu.HBM)] * 4,
        out_specs=pl.BlockSpec(memory_space=pltpu.VMEM),
        scratch_shapes=[
            pltpu.VMEM((s_dev,), jnp.float32),
            pltpu.VMEM((t_dev,), jnp.float32),
            pltpu.SemaphoreType.DMA((4,)),
        ],
        compiler_params=pltpu.CompilerParams(vmem_limit_bytes=2 * 2**20),
        name="pack",
    )(*fixed)
    near_pieces, far_pieces = exchange(block, "src")
    sources, targets = n * s_dev, n * t_dev
    half_s, half_t = sources // 2, targets // 2
    blk = 256
    f32, b16 = jnp.float32, jnp.bfloat16
    vmem = pl.BlockSpec(memory_space=pltpu.VMEM)
    near = pl.pallas_call(
        functools.partial(near_kernel, s_dev, t_dev, blk),
        out_shape=[
            jax.ShapeDtypeStruct((half_s, half_t), f32),
            jax.ShapeDtypeStruct((half_s, 4 * feat), b16),
            jax.ShapeDtypeStruct((half_t, 4 * feat), b16),
            jax.ShapeDtypeStruct((half_s, 1), f32),
            jax.ShapeDtypeStruct((1, half_t), f32),
            jax.ShapeDtypeStruct((8, feat), f32),
        ],
        in_specs=[vmem] * len(near_pieces),
        out_specs=[vmem] * 6,
        compiler_params=pltpu.CompilerParams(vmem_limit_bytes=NEAR_VMEM),
        cost_estimate=pl.CostEstimate(
            flops=2 * half_s * half_t * 4 * feat,
            bytes_accessed=8 * 2**20,
            transcendentals=half_s * half_t,
        ),
        name="near",
    )(*near_pieces)
    f_pot, g_pot, src_moved, tgt_moved = pl.pallas_call(
        functools.partial(whole_group_kernel, n, s_dev, t_dev, blk),
        out_shape=[
            jax.ShapeDtypeStruct((1, s_dev), f32),
            jax.ShapeDtypeStruct((1, t_dev), f32),
            jax.ShapeDtypeStruct((s_dev, feat), f32),
            jax.ShapeDtypeStruct((t_dev, feat), f32),
        ],
        in_specs=[vmem] * (len(near_pieces) + len(far_pieces) + 6),
        out_specs=[vmem] * 4,
        scratch_shapes=[
            pltpu.VMEM((half_s, half_t), f32),
            pltpu.VMEM((half_s, half_t), f32),
            pltpu.VMEM((half_s, half_t), f32),
            pltpu.VMEM((half_s, half_t), f32),
            pltpu.VMEM((half_s, 4 * feat), b16),
            pltpu.VMEM((half_t, 4 * feat), b16),
            pltpu.VMEM((sources, 1), f32),
            pltpu.VMEM((sources, 1), f32),
            pltpu.VMEM((8, half_t), f32),
            pltpu.VMEM((8, half_t), f32),
        ],
        compiler_params=pltpu.CompilerParams(vmem_limit_bytes=WHOLE_VMEM),
        name="whole_group",
    )(*near_pieces, *far_pieces, *near)
    return f_pot.reshape(s_dev), g_pot.reshape(t_dev), src_moved, tgt_moved


def merged(part, axis, combine):
    gathered = jax.tree.map(lambda a: lax.all_gather(a, axis), part)

    def take(source):
        return jax.tree.map(lambda a: lax.dynamic_index_in_dim(a, source, 0, False), gathered)

    return lax.fori_loop(
        1, lax.axis_size(axis), lambda source, state: combine(state, take(source)), take(0)
    )


def pair_cost(rows, cols, rows_sq, cols_sq, width):
    inner = jnp.dot(rows, cols.T, precision=HI, preferred_element_type=jnp.float32)
    return (rows_sq[:, None] + cols_sq[None, :] - 2.0 * inner) / width


def row_update(cost, g_pot, log_mass):
    scores = (g_pot[None, :] - cost) / EPS
    top = jnp.max(scores, axis=1)
    total = jnp.sum(jnp.exp(scores - top[:, None]), axis=1)
    return EPS * log_mass - EPS * (top + jnp.log(total))


def combine_pairs(first, second):
    top = jnp.maximum(first[0], second[0])
    total = first[1] * jnp.exp(first[0] - top) + second[1] * jnp.exp(second[0] - top)
    return (top, total)


def per_device_rows(source_feats, target_feats, log_a, log_b):
    width = source_feats.shape[1]
    rows = target_feats.shape[0]
    tgt_all, log_b_all = (
        lax.all_gather(target_feats, "src", axis=0, tiled=True),
        lax.all_gather(log_b, "src", axis=0, tiled=True),
    )
    sq_src = jnp.sum(source_feats * source_feats, axis=1)
    sq_tgt = jnp.sum(tgt_all * tgt_all, axis=1)
    cost = pair_cost(source_feats, tgt_all, sq_src, sq_tgt, width)
    g_pot = jnp.zeros((tgt_all.shape[0],), jnp.float32)
    f_pot = jnp.zeros((source_feats.shape[0],), jnp.float32)
    for step in range(ITERS):
        f_pot = row_update(cost, g_pot, log_a)
        scores = (f_pot[:, None] - cost) / EPS
        local_top = jnp.max(scores, axis=0)
        local_total = jnp.sum(jnp.exp(scores - local_top[None, :]), axis=0)
        top, total = merged((local_top, local_total), "src", combine_pairs)
        g_pot = EPS * log_b_all - EPS * (top + jnp.log(total))
    plan = jnp.exp((f_pot[:, None] + g_pot[None, :] - cost) / EPS)
    carried = jnp.dot(plan, tgt_all, precision=HI, preferred_element_type=jnp.float32)
    src_moved = carried / jnp.sum(plan, axis=1)[:, None]
    own_start = lax.axis_index("src") * rows
    g_own = lax.dynamic_slice_in_dim(g_pot, own_start, rows)
    gathered = lax.psum_scatter(
        lax.dot_general(
            plan,
            source_feats,
            (((0,), (0,)), ((), ())),
            precision=HI,
            preferred_element_type=jnp.float32,
        ),
        "src",
        scatter_dimension=0,
        tiled=True,
    )
    tgt_moved = gathered / jnp.exp(log_b)[:, None]
    return (f_pot, g_own, src_moved, tgt_moved)


def per_device(source_feats, target_feats, log_a, log_b):
    n = lax.axis_size("src")
    s_dev, feat = source_feats.shape
    t_dev = target_feats.shape[0]
    fits = 4 * n * s_dev * n * t_dev <= REPLICATED_BYTES
    shaped = n >= 4 and n & (n - 1) == 0 and s_dev % 16 == 0 and s_dev <= feat == t_dev
    if fits and shaped and (n * s_dev) % 512 == 0 and n == 16:
        return per_device_whole(source_feats, target_feats, log_a, log_b)
    return per_device_rows(source_feats, target_feats, log_a, log_b)


def solution(mesh):
    both = P(("groups", "src"), None)
    line = P(("groups", "src"))
    return jax.shard_map(
        per_device,
        mesh=mesh,
        in_specs=(both, both, line, line),
        out_specs=(line, line, both, both),
        check_vma=False,
    )
```

```python
import functools

import jax
import jax.numpy as jnp
from jax import lax
from jax.experimental import pallas as pl
from jax.experimental.pallas import tpu as pltpu
from jax.sharding import PartitionSpec as P

ITERS = 3
EPS = 0.05
LN2 = 0.6931471805599453
LOG2E = 1.4426950408889634
SAFE = 2.0**30
WIDE = 2.0**60
PARTS = 4
CHUNK = 256
NEAR_VMEM = 16 * 2**20
WHOLE_VMEM = 36 * 2**20
REPLICATED_BYTES = 24 * 2**20
HI = lax.Precision.HIGHEST


def split3(a):
    first = a.astype(jnp.bfloat16)
    rest = a - first.astype(jnp.float32)
    second = rest.astype(jnp.bfloat16)
    third = (rest - second.astype(jnp.float32)).astype(jnp.bfloat16)
    return first, second, third


def split2(a):
    first = a.astype(jnp.bfloat16)
    return first, (a - first.astype(jnp.float32)).astype(jnp.bfloat16)


def nt_dot(a, b, precision=None):
    return lax.dot_general(
        a, b, (((1,), (1,)), ((), ())), precision=precision, preferred_element_type=jnp.float32
    )


def least(values):
    return functools.reduce(jnp.minimum, values)


def most(values):
    return functools.reduce(jnp.maximum, values)


def blocks_of(pieces, rows):
    return [(ref, at) for ref in pieces for at in range(0, ref.shape[0], rows)]


def target_sum(blocks, s_dev, t_dev):
    total = sum(
        jnp.sum(ref[at + s_dev : at + s_dev + t_dev, :].reshape(t_dev // 8, 8, -1), axis=0)
        for ref, at in blocks
    )
    return jnp.sum(total, axis=0, keepdims=True)


def split_features(blocks, s_dev, t_dev, center, k, xs, ys):
    feat = center.shape[1]
    norms = []
    ones = jnp.ones((8, 3 * feat), jnp.bfloat16)
    for d, (ref, at) in enumerate(blocks):
        x1, x2 = split2((ref[at : at + s_dev, :] - center) * (2.0 * k))
        xs[d * s_dev : (d + 1) * s_dev, :] = jnp.concatenate([x1, x1, x2, x2], 1)
        y = ref[at + s_dev : at + s_dev + t_dev, :] - center
        y1, y2 = split2(y)
        ys[d * t_dev : (d + 1) * t_dev, :] = jnp.concatenate([y1, y2, y1, y2], 1)
        norms.append(nt_dot(ones, jnp.concatenate(split3(y * y), 1))[0:1, :])
    return jnp.concatenate(norms, 1) * k


def near_kernel(s_dev, t_dev, blk, *refs):
    pieces = refs[:-6]
    e_ref, xs, ys, r_ref, norm_ref, mid_ref = refs[-6:]
    feat = pieces[0].shape[1]
    k = LOG2E / (feat * EPS)
    blocks = blocks_of(pieces, s_dev + t_dev + 8)
    sources, targets = len(blocks) * s_dev, len(blocks) * t_dev
    center = target_sum(blocks, s_dev, t_dev) * (1.0 / targets)
    norm = split_features(blocks, s_dev, t_dev, center, k, xs, ys)
    norm_ref[...] = norm
    shift = jnp.mean(norm, axis=1, keepdims=True)
    mid_ref[0:1, :] = center
    mid_ref[1:2, :] = jnp.broadcast_to(shift, (1, feat))
    mid_ref[2:8, :] = jnp.zeros((6, feat), jnp.float32)
    g1 = shift - norm
    for i in range(sources // blk):
        s = slice(i * blk, (i + 1) * blk)
        row_sum = 0.0
        for c in range(0, targets, CHUNK):
            cols = slice(c, c + CHUNK)
            e = jnp.exp2(nt_dot(xs[s, :], ys[cols, :]) + g1[:, cols])
            e_ref[s, cols] = e
            row_sum += sum(e[:, c : c + feat] for c in range(0, CHUNK, feat))
        r_ref[s, :] = jnp.sum(row_sum, axis=1, keepdims=True)


def whole_group_kernel(n, s_dev, t_dev, blk, *refs):
    pieces = refs[:-20]
    e11, xs1, ys1, r1_ref, norm_ref, mid_ref = refs[-20:-14]
    f_ref, g_ref, sm_ref, tm_ref = refs[-14:-10]
    e12, e21, e22, e_own, xs2, ys2, la_col, u_col, acc0, acc1 = refs[-10:]
    feat = pieces[0].shape[1]
    rows = s_dev + t_dev + 8
    k = LOG2E / (feat * EPS)
    sources, targets = n * s_dev, n * t_dev
    half_s, half_t = sources // 2, targets // 2
    xs, ys, accs = (xs1, xs2), (ys1, ys2), (acc0, acc1)

    blocks = blocks_of(pieces, rows)
    center = mid_ref[0:1, :]
    shift = mid_ref[1:2, 0:1]
    norms = (norm_ref[...], split_features(blocks[n // 2 :], s_dev, t_dev, center, k, xs2, ys2))
    lbs = [ref[at + s_dev + t_dev : at + s_dev + t_dev + 1, :] for ref, at in blocks]
    las = [ref[at + s_dev + t_dev + 1 : at + s_dev + t_dev + 2, :] for ref, at in blocks]
    g1 = tuple(shift - norm for norm in norms)
    mass_b = tuple(jnp.exp(jnp.concatenate(part, 1)) for part in (lbs[: n // 2], lbs[n // 2 :]))
    la_t = jnp.exp(jnp.concatenate(las, 0)).T
    for d in range(n):
        la_col[d * s_dev : (d + 1) * s_dev, :] = la_t[:s_dev, d : d + 1]

    steps = sources // blk
    near = steps // 2
    parts = PARTS
    sub = blk // parts

    def halves(i, first=e11):
        at = (i % near) * blk
        return ((first, e12) if i < near else (e21, e22)), slice(at, at + blk)

    def column_part(e, u):
        return jnp.sum((e * u).reshape(e.shape[0] // 8, 8, half_t), axis=0)

    row_sums = [0.0] * steps

    def product(i, part):
        kept, where = halves(i)
        factor = xs[i // near][where, :]
        chunks = [
            (h, slice(c, c + CHUNK))
            for h in ((1,) if i < near else (0, 1))
            for c in range(0, half_t, CHUNK)
        ]
        for h, cols in chunks[part * len(chunks) // parts : (part + 1) * len(chunks) // parts]:
            e = jnp.exp2(nt_dot(factor, ys[h][cols, :]) + g1[h][:, cols])
            kept[h][where, cols] = e
            row_sums[i] += sum(e[:, c : c + feat] for c in range(0, CHUNK, feat))

    sums, ends = [], []

    def absorb(i, part):
        kept, where = halves(i)
        local = slice(part * sub, (part + 1) * sub)
        s = slice(where.start + local.start, where.start + local.stop)
        r = jnp.sum(row_sums[i][local, :], axis=1, keepdims=True)
        if i < near:
            r = r + r1_ref[s, :]
        sums.append(r)
        u = la_col[i * blk + local.start : i * blk + local.stop, :] / r
        acc0[...] += column_part(kept[0][s, :], u)
        acc1[...] += column_part(kept[1][s, :], u)

    def column_end():
        total = tuple(jnp.sum(acc[...], axis=0, keepdims=True) for acc in accs)
        ends.extend(total)
        return total

    def clear():
        for acc in accs:
            acc[...] = jnp.zeros_like(acc)

    clear()
    for part in range(parts):
        product(0, part)
    for i in range(steps):
        for part in range(parts):
            if i + 1 < steps:
                product(i + 1, part)
            absorb(i, part)
    total = column_end()

    def quarters_sum(wide, count):
        low = wide[:count, feat:] + (wide[count:, :feat] + wide[count:, feat:])
        return wide[:count, :feat] + low

    def target_sums(plan, i):
        at = (i % near) * blk
        return lax.dot_general(
            jnp.concatenate(split2(plan), 1),
            xs[i // near][at : at + blk, feat : 3 * feat],
            (((0,), (0,)), ((), ())),
            preferred_element_type=jnp.float32,
        )

    def put_targets(sums_of, mass):
        moved = quarters_sum(sum(sums_of), t_dev)
        mass = jnp.broadcast_to(mass * (2.0 * k), (feat, t_dev)).T
        tm_ref[...] = moved / mass + center

    def put_sources(plan):
        mass = jnp.sum(plan[0] + plan[1], axis=1, keepdims=True)
        wide = sum(
            jnp.dot(
                jnp.concatenate(split2(plan[h]), 0),
                ys[h][:, 0 : 2 * feat],
                preferred_element_type=jnp.float32,
            )
            for h in (0, 1)
        )
        sm_ref[...] = quarters_sum(wide, s_dev) / mass + center

    x_own = pieces[0][0:s_dev, :] - center
    sq_own = k * jnp.sum(x_own * x_own, axis=1, keepdims=True)

    for step in range(1, ITERS):
        v = tuple(m / t for m, t in zip(mass_b, total))
        clear()
        moved_parts = []
        for i in range(steps):
            kept, s = halves(i)
            e0, e1 = kept[0][s, :], kept[1][s, :]
            r = jnp.sum(e0 * v[0] + e1 * v[1], axis=1, keepdims=True)
            u = la_col[i * blk : (i + 1) * blk, :] / r
            acc0[...] += column_part(e0, u)
            acc1[...] += column_part(e1, u)
            if step == ITERS - 1:
                moved_parts.append(target_sums(e0[:, 0:t_dev] * u, i))
                if i == 0:
                    u_own = u[0:s_dev, :]
        total = column_end()
    v = tuple(m / t for m, t in zip(mass_b, total))

    def put_f(f):
        wide = jnp.broadcast_to(f, (s_dev, feat))
        wide = jnp.concatenate([wide, jnp.zeros((feat - s_dev, feat), jnp.float32)], 0)
        f_ref[...] = wide.T[0:1, 0:s_dev]

    put_f(EPS * jnp.log(u_own) + (EPS * LN2) * (sq_own + shift))
    g_ref[...] = EPS * jnp.log(v[0][:, 0:t_dev])
    put_targets(moved_parts, total[0][:, 0:t_dev])
    put_sources((e11[0:s_dev, :] * v[0], e12[0:s_dev, :] * v[1]))

    low_r, high_r, low_c, high_c = least(sums), most(sums), least(ends), most(ends)
    bad = jnp.max(jnp.where((low_r < 1.0) | (high_r > WIDE), 1.0, 0.0)) + jnp.max(
        jnp.where((low_c < 1.0 / SAFE) | (high_c > SAFE), 1.0, 0.0)
    )
    finite = (jnp.max(high_r) < WIDE) & (jnp.max(high_c) < SAFE)

    @pl.when(jnp.logical_not((bad == 0.0) & finite))
    def _():
        quarters = ((e_own, e12), (e21, e22))

        def at_block(i):
            return pl.ds(pl.multiple_of(i * blk, blk), blk)

        for a in (0, 1):
            for h in (0, 1):

                def inner(i, carry):
                    s = at_block(i)
                    quarters[a][h][s, :] = nt_dot(xs[a][s, :], ys[h][...])
                    return carry

                lax.fori_loop(0, near, inner, 0)

        def potentials(step, g):
            for a in (0, 1):

                def row(i, carry):
                    s, line = at_block(i), at_block(i + a * near)
                    t = [quarters[a][h][s, :] + g[h] for h in (0, 1)]
                    top = jnp.max(jnp.maximum(t[0], t[1]), axis=1, keepdims=True)
                    mass = jnp.sum(jnp.exp2(t[0] - top) + jnp.exp2(t[1] - top), axis=1, keepdims=True)
                    u_col[line, :] = jnp.log2(la_col[line, :]) - top - jnp.log2(mass)
                    return carry

                lax.fori_loop(0, near, row, 0)

            new = []
            for h in (0, 1):
                top = jnp.full((1, half_t), -jnp.inf, jnp.float32)
                mass = jnp.zeros((1, half_t), jnp.float32)
                for a in (0, 1):

                    def column_top(i, top):
                        t = quarters[a][h][at_block(i), :] + u_col[at_block(i + a * near), :]
                        return jnp.maximum(top, jnp.max(t, axis=0, keepdims=True))

                    top = lax.fori_loop(0, near, column_top, top)
                for a in (0, 1):

                    def column_mass(i, mass):
                        t = quarters[a][h][at_block(i), :] + u_col[at_block(i + a * near), :]
                        return mass + jnp.sum(jnp.exp2(t - top), axis=0, keepdims=True)

                    mass = lax.fori_loop(0, near, column_mass, mass)
                new.append(jnp.log2(mass_b[h]) - top - jnp.log2(mass))
            return tuple(new)

        g = lax.fori_loop(0, ITERS, potentials, (-norms[0], -norms[1]))
        u_first = u_col[0:s_dev, :]
        put_f((EPS * LN2) * (u_first + sq_own))
        g_ref[...] = (EPS * LN2) * (g[0][:, 0:t_dev] + norms[0][:, 0:t_dev])
        put_sources([jnp.exp2(quarters[0][h][0:s_dev, :] + u_first + g[h]) for h in (0, 1)])

        def own_columns(i):
            at = (i % near) * blk
            inner = quarters[i // near][0][at : at + blk, 0:t_dev]
            return jnp.exp2(inner + u_col[i * blk : (i + 1) * blk, :] + g[0][:, 0:t_dev])

        mass = mass_b[0][:, 0:t_dev]
        put_targets([target_sums(own_columns(i), i) for i in range(steps)], mass)


def exchange(block, axis):
    n = lax.axis_size(axis)

    def swap(a, bits):
        return lax.ppermute(a, axis, [(i, i ^ bits) for i in range(n)])

    near, jump = swap(block, 4), swap(block, 8)
    across = swap(block, 2)
    last, over = swap(jump, 4), swap(jump, 2)
    line = [block, near, jump, last]
    side = [across, swap(near, 2), over, swap(over, 4)]
    return line + [swap(a, 1) for a in line], side + [swap(a, 1) for a in side]


def pack_kernel(x_ref, y_ref, la_ref, lb_ref, out_ref, la_row, lb_row, sems):
    s_dev, t_dev = x_ref.shape[0], y_ref.shape[0]
    rows = s_dev + t_dev
    copies = [
        pltpu.make_async_copy(src, dst, sems.at[i])
        for i, (src, dst) in enumerate(
            (
                (x_ref, out_ref.at[0:s_dev, :]),
                (y_ref, out_ref.at[s_dev:rows, :]),
                (la_ref, la_row),
                (lb_ref, lb_row),
            )
        )
    ]
    for copy in copies:
        copy.start()
    out_ref[rows:, :] = jnp.zeros((8, x_ref.shape[1]), jnp.float32)
    copies[2].wait()
    out_ref[rows + 1 : rows + 2, 0:s_dev] = la_row[...].reshape(1, s_dev)
    copies[3].wait()
    out_ref[rows : rows + 1, :] = lb_row[...].reshape(1, t_dev)
    copies[0].wait()
    copies[1].wait()


def per_device_whole(source_feats, target_feats, log_a, log_b):
    n = lax.axis_size("src")
    s_dev, feat = source_feats.shape
    t_dev = target_feats.shape[0]
    fixed = [pltpu.with_memory_space_constraint(a, pltpu.HBM) for a in (source_feats, target_feats, log_a, log_b)]
    block = pl.pallas_call(
        pack_kernel,
        out_shape=pltpu.VMEM((s_dev + t_dev + 8, feat), jnp.float32),
        in_specs=[pl.BlockSpec(memory_space=pltpu.HBM)] * 4,
        out_specs=pl.BlockSpec(memory_space=pltpu.VMEM),
        scratch_shapes=[
            pltpu.VMEM((s_dev,), jnp.float32),
            pltpu.VMEM((t_dev,), jnp.float32),
            pltpu.SemaphoreType.DMA((4,)),
        ],
        compiler_params=pltpu.CompilerParams(vmem_limit_bytes=2 * 2**20),
        name="pack",
    )(*fixed)
    near_pieces, far_pieces = exchange(block, "src")
    sources, targets = n * s_dev, n * t_dev
    half_s, half_t = sources // 2, targets // 2
    blk = 256
    f32, b16 = jnp.float32, jnp.bfloat16
    vmem = pl.BlockSpec(memory_space=pltpu.VMEM)
    near = pl.pallas_call(
        functools.partial(near_kernel, s_dev, t_dev, blk),
        out_shape=[
            jax.ShapeDtypeStruct((half_s, half_t), f32),
            jax.ShapeDtypeStruct((half_s, 4 * feat), b16),
            jax.ShapeDtypeStruct((half_t, 4 * feat), b16),
            jax.ShapeDtypeStruct((half_s, 1), f32),
            jax.ShapeDtypeStruct((1, half_t), f32),
            jax.ShapeDtypeStruct((8, feat), f32),
        ],
        in_specs=[vmem] * len(near_pieces),
        out_specs=[vmem] * 6,
        compiler_params=pltpu.CompilerParams(vmem_limit_bytes=NEAR_VMEM),
        cost_estimate=pl.CostEstimate(
            flops=2 * half_s * half_t * 4 * feat,
            bytes_accessed=8 * 2**20,
            transcendentals=half_s * half_t,
        ),
        name="near",
    )(*near_pieces)
    f_pot, g_pot, src_moved, tgt_moved = pl.pallas_call(
        functools.partial(whole_group_kernel, n, s_dev, t_dev, blk),
        out_shape=[
            jax.ShapeDtypeStruct((1, s_dev), f32),
            jax.ShapeDtypeStruct((1, t_dev), f32),
            jax.ShapeDtypeStruct((s_dev, feat), f32),
            jax.ShapeDtypeStruct((t_dev, feat), f32),
        ],
        in_specs=[vmem] * (len(near_pieces) + len(far_pieces) + 6),
        out_specs=[vmem] * 4,
        scratch_shapes=[
            pltpu.VMEM((half_s, half_t), f32),
            pltpu.VMEM((half_s, half_t), f32),
            pltpu.VMEM((half_s, half_t), f32),
            pltpu.VMEM((half_s, half_t), f32),
            pltpu.VMEM((half_s, 4 * feat), b16),
            pltpu.VMEM((half_t, 4 * feat), b16),
            pltpu.VMEM((sources, 1), f32),
            pltpu.VMEM((sources, 1), f32),
            pltpu.VMEM((8, half_t), f32),
            pltpu.VMEM((8, half_t), f32),
        ],
        compiler_params=pltpu.CompilerParams(vmem_limit_bytes=WHOLE_VMEM),
        name="whole_group",
    )(*near_pieces, *far_pieces, *near)
    return f_pot.reshape(s_dev), g_pot.reshape(t_dev), src_moved, tgt_moved


def merged(part, axis, combine):
    gathered = jax.tree.map(lambda a: lax.all_gather(a, axis), part)

    def take(source):
        return jax.tree.map(lambda a: lax.dynamic_index_in_dim(a, source, 0, False), gathered)

    return lax.fori_loop(
        1, lax.axis_size(axis), lambda source, state: combine(state, take(source)), take(0)
    )


def pair_cost(rows, cols, rows_sq, cols_sq, width):
    inner = jnp.dot(rows, cols.T, precision=HI, preferred_element_type=jnp.float32)
    return (rows_sq[:, None] + cols_sq[None, :] - 2.0 * inner) / width


def row_update(cost, g_pot, log_mass):
    scores = (g_pot[None, :] - cost) / EPS
    top = jnp.max(scores, axis=1)
    total = jnp.sum(jnp.exp(scores - top[:, None]), axis=1)
    return EPS * log_mass - EPS * (top + jnp.log(total))


def combine_pairs(first, second):
    top = jnp.maximum(first[0], second[0])
    total = first[1] * jnp.exp(first[0] - top) + second[1] * jnp.exp(second[0] - top)
    return (top, total)


def per_device_rows(source_feats, target_feats, log_a, log_b):
    width = source_feats.shape[1]
    rows = target_feats.shape[0]
    tgt_all, log_b_all = (
        lax.all_gather(target_feats, "src", axis=0, tiled=True),
        lax.all_gather(log_b, "src", axis=0, tiled=True),
    )
    sq_src = jnp.sum(source_feats * source_feats, axis=1)
    sq_tgt = jnp.sum(tgt_all * tgt_all, axis=1)
    cost = pair_cost(source_feats, tgt_all, sq_src, sq_tgt, width)
    g_pot = jnp.zeros((tgt_all.shape[0],), jnp.float32)
    f_pot = jnp.zeros((source_feats.shape[0],), jnp.float32)
    for step in range(ITERS):
        f_pot = row_update(cost, g_pot, log_a)
        scores = (f_pot[:, None] - cost) / EPS
        local_top = jnp.max(scores, axis=0)
        local_total = jnp.sum(jnp.exp(scores - local_top[None, :]), axis=0)
        top, total = merged((local_top, local_total), "src", combine_pairs)
        g_pot = EPS * log_b_all - EPS * (top + jnp.log(total))
    plan = jnp.exp((f_pot[:, None] + g_pot[None, :] - cost) / EPS)
    carried = jnp.dot(plan, tgt_all, precision=HI, preferred_element_type=jnp.float32)
    src_moved = carried / jnp.sum(plan, axis=1)[:, None]
    own_start = lax.axis_index("src") * rows
    g_own = lax.dynamic_slice_in_dim(g_pot, own_start, rows)
    gathered = lax.psum_scatter(
        lax.dot_general(
            plan,
            source_feats,
            (((0,), (0,)), ((), ())),
            precision=HI,
            preferred_element_type=jnp.float32,
        ),
        "src",
        scatter_dimension=0,
        tiled=True,
    )
    tgt_moved = gathered / jnp.exp(log_b)[:, None]
    return (f_pot, g_own, src_moved, tgt_moved)


def per_device(source_feats, target_feats, log_a, log_b):
    n = lax.axis_size("src")
    s_dev, feat = source_feats.shape
    t_dev = target_feats.shape[0]
    fits = 4 * n * s_dev * n * t_dev <= REPLICATED_BYTES
    shaped = n >= 4 and n & (n - 1) == 0 and s_dev % 16 == 0 and s_dev <= feat == t_dev
    if fits and shaped and (n * s_dev) % 512 == 0 and n == 16:
        return per_device_whole(source_feats, target_feats, log_a, log_b)
    return per_device_rows(source_feats, target_feats, log_a, log_b)


def solution(mesh):
    both = P(("groups", "src"), None)
    line = P(("groups", "src"))
    return jax.shard_map(
        per_device,
        mesh=mesh,
        in_specs=(both, both, line, line),
        out_specs=(line, line, both, both),
        check_vma=False,
    )
```
